32 devices in a mesh: dp: 4 (over y, x), ctx: 8 (over z, core).
Axes of the slice: x: 2, y: 2, z: 4, core: 2. Of those that a mesh axis runs over, the one named last changes fastest.
Arguments:
- queries: bfloat16 [5120, 4096], P(('dp', 'ctx')), may hold values from -20 to 20
- keys: bfloat16 [5120, 512], P(('dp', 'ctx')), may hold values from -6 to 6
- values: bfloat16 [5120, 512], P(('dp', 'ctx')), may hold values from -6 to 6
- output_gradient: bfloat16 [5120, 4096], P(('dp', 'ctx')), may hold values from -24 to 24
- adapter_rank_cotangent: bfloat16 [5120, 32], P(('dp', 'ctx')), may hold values from -64 to 64
- adapter_down_weight: bfloat16 [4096, 32], replicated, may hold values from -0.09375 to 0.09375
- relay_owner_index: int32 [32, 64], P(('dp', 'ctx')), may hold values from 0 to 7, as said below
- relay_block_slot: int32 [32, 64], P(('dp', 'ctx')), may hold values from 0 to 63, as said below
- short_rollout_lengths: int32 [32, 4], P(('dp', 'ctx')), may hold values from 1 to 16, 32 in all within a row
Outputs:
- owner_query_gradient: bfloat16 [5120, 4096], P(('dp', 'ctx'))
- owner_key_gradient: bfloat16 [5120, 512], P(('dp', 'ctx'))
- owner_value_gradient: bfloat16 [5120, 512], P(('dp', 'ctx'))
- adapter_down_gradient: float32 [4096, 32], P(('dp', 'ctx'))
The draws below stay inside these ranges and needn't reach their ends.
Inputs may be any that keep to these rules, and one draw needn't show every extreme that they name: `relay_owner_index`: blocks stay on their line (same data index). Every owner receives exactly 64 blocks, at most 12 from one device, and on every line some device sends exactly 12 blocks to one owner. On each line the pairs (relay_owner_index, relay_block_slot) are all different.
All inputs are finite; a program needn't handle non-finite values.
Results may differ from the reference program's by a relative error of at most 0.0093.
Values may be sent and summed in bfloat16 or wider, within the bound.
A program may use at most 128 MiB of HBM per device.

```python
import math
import jax
import jax.numpy as jnp
import numpy as np
from jax import lax

HEAD_SIZE = 128
QUERY_HEADS = 32
KVH = 4
GROUP = 8
ADAPTER_RANK = 32
LONG_DEVICE_ROWS = 128
SHORT_DEV = 32
SUB = 4
BLK = 2
NSEG = 4
LINE = 8
NDEV = 32
NB = 64
DEVICE_ROWS = 160
TOTAL_ROWS = 5120
SMOST = 16


def plan_tables(key):
    mean_count = NB // LINE
    half_count = mean_count // 2

    def one_line(line_key):
        keys_here = jax.random.split(line_key, 5)
        pairing = jax.random.permutation(keys_here[0], LINE)
        extra = jax.random.randint(keys_here[1], (LINE // 2,), 0, half_count + 1)
        extra = extra.at[0].set(half_count)
        counts = jnp.zeros((LINE,), jnp.int32)
        counts = counts.at[pairing[0::2]].set(mean_count + extra)
        counts = counts.at[pairing[1::2]].set(mean_count - extra)
        ends = jnp.cumsum(counts)
        block_ids = jnp.arange(NB, dtype=jnp.int32)
        offset = jnp.sum((ends[None, :] <= block_ids[:, None]).astype(jnp.int32), axis=1)
        relabel = jax.random.permutation(keys_here[2], LINE)
        sources = jnp.arange(LINE, dtype=jnp.int32)
        dest = relabel[(sources[:, None] + offset[None, :]) % LINE]
        slot_perms = jax.vmap(lambda inner: jax.random.permutation(inner, NB))(jax.random.split(keys_here[3], LINE))
        slot_by_order = slot_perms[dest, block_ids[None, :]]
        block_perms = jax.vmap(lambda inner: jax.random.permutation(inner, NB))(jax.random.split(keys_here[4], LINE))
        order_of_block = jnp.argsort(block_perms, axis=1)
        owner = jnp.take_along_axis(dest, order_of_block, axis=1)
        slot = jnp.take_along_axis(slot_by_order, order_of_block, axis=1)
        return (owner.astype(jnp.int32), slot.astype(jnp.int32))
    owners, slots = jax.vmap(one_line)(jax.random.split(key, NDEV // LINE))
    return (owners.reshape(NDEV, NB), slots.reshape(NDEV, NB))


def draw_relay_owner_index(key, part):
    owner, slot = plan_tables(key)
    return owner


def draw_relay_block_slot(key, part):
    owner, slot = plan_tables(key)
    return slot


def draw_keys(key, part):
    key = jax.random.fold_in(key, 5)
    base = jax.random.truncated_normal(key, -6.0, 6.0, (TOTAL_ROWS, KVH * HEAD_SIZE), jnp.float32)
    return base.astype(jnp.bfloat16)


def draw_queries(key, part):
    key = jax.random.fold_in(key, 6)
    base = jax.random.truncated_normal(key, -6.0, 6.0, (TOTAL_ROWS, QUERY_HEADS * HEAD_SIZE), jnp.float32)
    return base.astype(jnp.bfloat16)


def levels(own_key, shape, cuts, low, top_value):
    def one(axis_at, shards_of):
        steps = jax.random.uniform(jax.random.fold_in(jax.random.fold_in(own_key, 6), axis_at), (shards_of,), jnp.float32, low / len(cuts), top_value / len(cuts))
        return jnp.repeat(jnp.exp(steps), shape[axis_at] // shards_of).reshape((-1,) + (1,) * (len(shape) - axis_at - 1))

    gain = one(*cuts[0])
    for cut in cuts[1:]:
        gain = gain * one(*cut)
    return gain


def split_up(count, total, most, skew):
    loads = [(1 << 20) // math.isqrt(grade ** skew) + 1 for grade in range(2, count + 1)]
    spare, holding = total - most - (count - 1), [1] * (count - 1)
    while spare > 0:
        movable = [i for i in range(count - 1) if holding[i] < most]
        whole, budget = sum([loads[i] for i in movable]), spare
        for i in movable:
            more = min(most - holding[i], max(1, budget * loads[i] // whole), spare)
            holding[i] = holding[i] + more
            spare = spare - more
    return np.array([most] + holding)


def uneven(rng, amount, total, limit, lean):
    if amount == 2:
        one = jax.random.randint(rng, (), max(1, total - limit), min(limit, total - 1) + 1)
        return jnp.stack([one, total - one])
    sizes = jnp.asarray(split_up(amount, total, limit, lean), jnp.int32)
    twos = (amount - 1) // 2
    source_of, taker = sizes[1:1 + 2 * twos:2], sizes[2:2 + 2 * twos:2]
    room = jnp.minimum(source_of - 1, limit - taker)
    shifted = jax.random.randint(jax.random.fold_in(rng, 1), (twos,), 0, 1 << 20) % (room + 1)
    sizes = sizes.at[1:1 + 2 * twos:2].set(source_of - shifted).at[2:2 + 2 * twos:2].set(taker + shifted)
    return sizes[jax.random.permutation(jax.random.fold_in(rng, 2), amount)]


def scatter_about(stream_key, extent, scale, most, pieces=(), held_as=jnp.bfloat16):
    values = jax.random.normal(stream_key, extent, jnp.float32) * scale
    if len(pieces) > 0:
        values = levels(stream_key, extent, pieces, -0.22, 0.18) * values
    return jnp.clip(values, min=-most, max=most).astype(held_as)


def setup_inputs(seed: int = 0) -> dict:
    key_of = jax.random.split(jax.random.key(seed), 10)
    return {
        "queries": draw_queries(jax.random.fold_in(key_of[9], 71), 0),
        "keys": draw_keys(jax.random.fold_in(key_of[9], 71), 0),
        "values": scatter_about(key_of[2], (TOTAL_ROWS, KVH * HEAD_SIZE), 1.0, 6.0, ((0, 32),)),
        "output_gradient": scatter_about(key_of[3], (TOTAL_ROWS, QUERY_HEADS * HEAD_SIZE), 4.0, 24.0, ((0, 32),)),
        "adapter_rank_cotangent": scatter_about(key_of[4], (TOTAL_ROWS, ADAPTER_RANK), 12.0, 64.0, ((0, 32),)),
        "adapter_down_weight": scatter_about(key_of[5], (QUERY_HEADS * HEAD_SIZE, ADAPTER_RANK), (QUERY_HEADS * HEAD_SIZE) ** -0.5, 0.09375),
        "relay_owner_index": draw_relay_owner_index(jax.random.fold_in(key_of[9], 71), 0),
        "relay_block_slot": draw_relay_block_slot(jax.random.fold_in(key_of[9], 71), 0),
        "short_rollout_lengths": jax.vmap(lambda own: uneven(own, NSEG, SHORT_DEV, SMOST, 2))(jax.random.split(key_of[8], NDEV)).reshape((NDEV, NSEG)).astype(jnp.int32),
    }


def relayed_block_rows(rows_all, relay_owner_index, relay_block_slot):
    width = rows_all.shape[1]
    shaped = rows_all.reshape(NDEV, DEVICE_ROWS, width)
    blocks = shaped[:, :LONG_DEVICE_ROWS].reshape(NDEV * NB, BLK, width)
    line_start = jnp.arange(NDEV, dtype=jnp.int32) // LINE * LINE
    target = ((line_start[:, None] + relay_owner_index.astype(jnp.int32)) * NB + relay_block_slot.astype(jnp.int32)).reshape(NDEV * NB)
    placed = jnp.zeros_like(blocks).at[target.astype(jnp.int32)].set(blocks)
    return (placed.reshape(NDEV, LONG_DEVICE_ROWS, width), shaped[:, LONG_DEVICE_ROWS:])

def short_rollout_mask(lengths):
    ends = jnp.cumsum(lengths.astype(jnp.int32))
    row_ids = jnp.arange(SHORT_DEV, dtype=jnp.int32)
    segment = lax.optimization_barrier(jnp.sum((ends[None, :] <= row_ids[:, None]).astype(jnp.int32), axis=1))
    return (segment[:, None] == segment[None, :]) & (row_ids[None, :] <= row_ids[:, None])

def attend_rows(query_block, key_block_rows, value_block_rows, output_cotangent, adapter_cotangent, adapter_down_weight, visible_mask):
    count = query_block.shape[0]
    scale = 1.0 / math.sqrt(HEAD_SIZE)
    query4 = query_block.astype(jnp.float32).reshape(count, KVH, GROUP, HEAD_SIZE)
    key3 = key_block_rows.astype(jnp.float32).reshape(count, KVH, HEAD_SIZE)
    value3 = value_block_rows.astype(jnp.float32).reshape(count, KVH, HEAD_SIZE)
    scores = jnp.einsum('ikgd,jkd->kgij', query4, key3) * scale
    best = lax.optimization_barrier(jnp.max(jnp.where(visible_mask, scores, -jnp.inf), axis=-1, keepdims=True))
    mass = lax.optimization_barrier(jnp.sum(jnp.where(visible_mask, jnp.exp(scores - best), 0.0), axis=-1, keepdims=True))
    log_total = best + jnp.log(mass)
    weights = jnp.where(visible_mask, jnp.exp(scores - log_total), 0.0).astype(jnp.bfloat16)
    weights = lax.optimization_barrier(weights).astype(jnp.float32)
    attended4 = jnp.einsum('kgij,jkd->ikgd', weights, value3)
    attended_b = attended4.reshape(count, QUERY_HEADS * HEAD_SIZE).astype(jnp.bfloat16)
    branch_choice = jnp.einsum('fe,ve->fv', adapter_cotangent.astype(jnp.float32), adapter_down_weight.astype(jnp.float32))
    grad_out = (output_cotangent.astype(jnp.float32) + branch_choice).astype(jnp.bfloat16)
    grad4 = lax.optimization_barrier(grad_out).astype(jnp.float32).reshape(count, KVH, GROUP, HEAD_SIZE)
    dprob = jnp.einsum('ikgd,jkd->kgij', grad4, value3)
    delta = jnp.einsum('ikgd,ikgd->kgi', grad4, attended4)[..., None]
    dscore = (weights * (dprob - delta) * scale).astype(jnp.bfloat16)
    dscore = lax.optimization_barrier(dscore).astype(jnp.float32)
    query_gradient = jnp.einsum('kgij,jkd->ikgd', dscore, key3).reshape(count, QUERY_HEADS * HEAD_SIZE).astype(jnp.bfloat16)
    key_gradient = jnp.einsum('kgij,ikgd->jkd', dscore, query4).reshape(count, KVH * HEAD_SIZE).astype(jnp.bfloat16)
    value_gradient = jnp.einsum('kgij,ikgd->jkd', weights, grad4).reshape(count, KVH * HEAD_SIZE).astype(jnp.bfloat16)
    gradient_term = jnp.dot(attended_b.T, adapter_cotangent, preferred_element_type=jnp.float32)
    return (query_gradient, key_gradient, value_gradient, gradient_term)

def reference(queries, keys, values, output_gradient, adapter_rank_cotangent, adapter_down_weight, relay_owner_index, relay_block_slot, short_rollout_lengths):
    moved_rows = [relayed_block_rows(single_entry, relay_owner_index, relay_block_slot) for single_entry in (queries, keys, values, output_gradient, adapter_rank_cotangent)]
    groups = NDEV // SUB
    span = SUB * LONG_DEVICE_ROWS
    long_parts = tuple((pair[0].reshape(groups, span, pair[0].shape[2]) for pair in moved_rows))
    short_parts = tuple((pair[1] for pair in moved_rows))
    positions = jnp.arange(span, dtype=jnp.int32)
    causal_mask = positions[None, :] <= positions[:, None]

    def long_step(carry, entry_list):
        query_gradient, key_gradient, value_gradient, gradient_term = attend_rows(entry_list[0], entry_list[1], entry_list[2], entry_list[3], entry_list[4], adapter_down_weight, causal_mask)
        return (carry + gradient_term, (query_gradient, key_gradient, value_gradient))

    def short_step(carry, entry_list):
        query_gradient, key_gradient, value_gradient, gradient_term = attend_rows(entry_list[0], entry_list[1], entry_list[2], entry_list[3], entry_list[4], adapter_down_weight, short_rollout_mask(entry_list[5]))
        return (carry + gradient_term, (query_gradient, key_gradient, value_gradient))
    zero_term = jnp.zeros((QUERY_HEADS * HEAD_SIZE, ADAPTER_RANK), jnp.float32)
    long_sum, long_out = lax.scan(long_step, zero_term, long_parts)
    total_value, short_out = lax.scan(short_step, long_sum, short_parts + (short_rollout_lengths,))
    output_list = []
    for long_piece, short_piece in zip(long_out, short_out):
        width = long_piece.shape[2]
        joined = jnp.concatenate([long_piece.reshape(NDEV, LONG_DEVICE_ROWS, width), short_piece], axis=1)
        output_list.append(joined.reshape(TOTAL_ROWS, width))
    adapter_down_gradient = total_value * (1.0 / math.sqrt(TOTAL_ROWS))
    return (output_list[0], output_list[1], output_list[2], adapter_down_gradient)
```

```python
import math

import jax
import jax.numpy as jnp
from jax import lax
from jax.experimental import pallas as pl
from jax.experimental.pallas import tpu as pltpu
from jax.sharding import PartitionSpec as P

HEAD_SIZE = 128
QUERY_HEADS = 32
KVH = 4
GROUP = 8
ADAPTER_RANK = 32
LONG_DEVICE_ROWS = 128
SHORT_DEV = 32
SUB = 4
BLK = 2
NB = 64
DEVICE_ROWS = 160


NEG_FILL = -1e30


def from_behind(shard, axis, by):
    count = lax.axis_size(axis)
    pairs = [(i, i + by) for i in range(count) if 0 <= i + by < count]
    return lax.ppermute(shard, axis, pairs)


def shifted(block, axis, distance):
    devices = range(lax.axis_size(axis))
    route = [((i - distance) % len(devices), i) for i in devices]
    return lax.ppermute(block, axis, route)


def head_scores(query4, key3):
    raw = jnp.einsum("ikgd,jkd->kgij", query4, key3, preferred_element_type=jnp.float32)
    return raw * (1.0 / math.sqrt(query4.shape[3]))


def running_stats(state, query4, key3, visible_mask):
    best, mass = state
    raw = head_scores(query4, key3)
    fresh = jnp.maximum(best, jnp.max(jnp.where(visible_mask, raw, NEG_FILL), axis=-1))
    mass = mass * jnp.exp(best - fresh) + jnp.sum(
        jnp.where(visible_mask, jnp.exp(raw - fresh[..., None]), 0.0), axis=-1
    )
    return (fresh, mass)


def block_weights(query4, key3, visible_mask, log_total):
    raw = head_scores(query4, key3)
    return jnp.where(visible_mask, jnp.exp(raw - log_total[..., None]), 0.0).astype(jnp.bfloat16)


def forward_values(attended, query4, key3, value3, visible_mask, log_total):
    weights = block_weights(query4, key3, visible_mask, log_total)
    return attended + jnp.einsum(
        "kgij,jkd->ikgd", weights, value3, preferred_element_type=jnp.float32
    )


def backward_block(query4, key3, value3, grad4, visible_mask, log_total, delta):
    weights = block_weights(query4, key3, visible_mask, log_total)
    dprob = jnp.einsum("ikgd,jkd->kgij", grad4, value3, preferred_element_type=jnp.float32)
    dscore = (
        weights.astype(jnp.float32)
        * (dprob - delta[..., None])
        * (1.0 / math.sqrt(query4.shape[3]))
    ).astype(jnp.bfloat16)
    part_q = jnp.einsum("kgij,jkd->ikgd", dscore, key3, preferred_element_type=jnp.float32)
    part_k = jnp.einsum("kgij,ikgd->jkd", dscore, query4, preferred_element_type=jnp.float32)
    part_v = jnp.einsum("kgij,ikgd->jkd", weights, grad4, preferred_element_type=jnp.float32)
    return (part_q, part_k, part_v)


def row_delta(grad4, attended):
    return jnp.einsum("ikgd,ikgd->kgi", grad4.astype(jnp.float32), attended)


def shards(
    queries,
    keys,
    values,
    output_gradient,
    adapter_rank_cotangent,
    adapter_down_weight,
    relay_owner_index,
    relay_block_slot,
    short_rollout_lengths,
):
    line_size = lax.axis_size("ctx")
    slots_each = 3 * NB // (2 * line_size)
    owners = relay_owner_index[0]
    targets = relay_block_slot[0]
    block_ids = jnp.arange(NB, dtype=jnp.int32)
    same_owner = owners[:, None] == owners[None, :]
    earlier = block_ids[None, :] < block_ids[:, None]
    within = jnp.sum((same_owner & earlier).astype(jnp.int32), axis=1)
    position = owners * slots_each + within
    buffer_ids = jnp.arange(line_size * slots_each, dtype=jnp.int32)
    matches = position[None, :] == buffer_ids[:, None]
    filled = jnp.any(matches, axis=1)
    source_ids = jnp.sum(jnp.where(matches, block_ids[None, :], 0), axis=1)
    carried = jnp.where(filled, jnp.sum(jnp.where(matches, targets[None, :], 0), axis=1), -1)

    def packed_rows(rows_in):
        blocks = rows_in[:LONG_DEVICE_ROWS].reshape(NB, BLK, rows_in.shape[1])
        chosen = jnp.take(blocks, source_ids, axis=0)
        return jnp.where(filled[:, None, None], chosen, jnp.zeros_like(chosen))

    arrived = (
        lax.all_to_all(packed_rows(queries), "ctx", split_axis=0, concat_axis=0, tiled=True),
        lax.all_to_all(packed_rows(keys), "ctx", split_axis=0, concat_axis=0, tiled=True),
        lax.all_to_all(packed_rows(values), "ctx", split_axis=0, concat_axis=0, tiled=True),
        lax.all_to_all(
            packed_rows(output_gradient), "ctx", split_axis=0, concat_axis=0, tiled=True
        ),
        lax.all_to_all(
            packed_rows(adapter_rank_cotangent), "ctx", split_axis=0, concat_axis=0, tiled=True
        ),
        lax.all_to_all(
            carried.astype(jnp.bfloat16), "ctx", split_axis=0, concat_axis=0, tiled=True
        ),
    )
    landing = arrived[5].astype(jnp.int32)
    pick_from = jnp.sum(
        jnp.where(landing[None, :] == block_ids[:, None], buffer_ids[None, :], 0), axis=1
    )

    def unpacked(received):
        return jnp.take(received, pick_from, axis=0).reshape(LONG_DEVICE_ROWS, received.shape[2])

    long_q = unpacked(arrived[0])
    long_k = unpacked(arrived[1])
    long_v = unpacked(arrived[2])
    long_d = unpacked(arrived[3])
    long_c = unpacked(arrived[4])

    def total_grad(output_cotangent, adapter_cotangent):
        branch_choice = jnp.einsum(
            "fe,ve->fv", adapter_cotangent, adapter_down_weight, preferred_element_type=jnp.float32
        )
        return (output_cotangent.astype(jnp.float32) + branch_choice).astype(jnp.bfloat16)

    short_q = queries[LONG_DEVICE_ROWS:].reshape(SHORT_DEV, KVH, GROUP, HEAD_SIZE)
    short_k = keys[LONG_DEVICE_ROWS:].reshape(SHORT_DEV, KVH, HEAD_SIZE)
    short_v = values[LONG_DEVICE_ROWS:].reshape(SHORT_DEV, KVH, HEAD_SIZE)
    short_cotangent = adapter_rank_cotangent[LONG_DEVICE_ROWS:]
    short_g = total_grad(output_gradient[LONG_DEVICE_ROWS:], short_cotangent).reshape(
        SHORT_DEV, KVH, GROUP, HEAD_SIZE
    )
    ends = jnp.cumsum(short_rollout_lengths[0])
    short_ids = jnp.arange(SHORT_DEV, dtype=jnp.int32)
    segment = jnp.sum((ends[None, :] <= short_ids[:, None]).astype(jnp.int32), axis=1)
    short_seen = (segment[:, None] == segment[None, :]) & (short_ids[None, :] <= short_ids[:, None])
    short_best = jnp.full((KVH, GROUP, SHORT_DEV), NEG_FILL, jnp.float32)
    short_best, short_mass = running_stats(
        (short_best, jnp.zeros_like(short_best)), short_q, short_k, short_seen
    )
    short_log = short_best + jnp.log(short_mass)
    short_att = forward_values(
        jnp.zeros((SHORT_DEV, KVH, GROUP, HEAD_SIZE), jnp.float32),
        short_q,
        short_k,
        short_v,
        short_seen,
        short_log,
    )
    short_delta = row_delta(short_g, short_att)
    short_dq, short_dk, short_dv = backward_block(
        short_q, short_k, short_v, short_g, short_seen, short_log, short_delta
    )
    query4 = long_q.reshape(LONG_DEVICE_ROWS, KVH, GROUP, HEAD_SIZE)
    key3 = long_k.reshape(LONG_DEVICE_ROWS, KVH, HEAD_SIZE)
    value3 = long_v.reshape(LONG_DEVICE_ROWS, KVH, HEAD_SIZE)
    grad4 = total_grad(long_d, long_c).reshape(LONG_DEVICE_ROWS, KVH, GROUP, HEAD_SIZE)
    member = lax.axis_index("ctx") % SUB
    row_ids = jnp.arange(LONG_DEVICE_ROWS, dtype=jnp.int32)

    def long_mask(hop_index):
        source = member - hop_index
        return (source >= 0) & (
            source * LONG_DEVICE_ROWS + row_ids[None, :]
            <= member * LONG_DEVICE_ROWS + row_ids[:, None]
        )

    best = jnp.full((KVH, GROUP, LONG_DEVICE_ROWS), NEG_FILL, jnp.float32)
    mass = jnp.zeros_like(best)
    stored = []
    key_now, value_now = (key3, value3)
    for hop_index in range(SUB):
        if hop_index > 0:
            key_now, value_now = from_behind((key_now, value_now), "ctx", 1)
        stored.append((key_now, value_now))
        best, mass = lax.cond(
            hop_index <= member,
            lambda state, kk=key_now, hh=hop_index: running_stats(state, query4, kk, long_mask(hh)),
            lambda state: state,
            (best, mass),
        )
    log_total = best + jnp.log(mass)
    attended = jnp.zeros((LONG_DEVICE_ROWS, KVH, GROUP, HEAD_SIZE), jnp.float32)
    key_now, value_now = (key3, value3)
    for hop_index in range(SUB):
        if hop_index > 0:
            key_now, value_now = from_behind((key_now, value_now), "ctx", 1)
        attended = lax.cond(
            hop_index <= member,
            lambda acc, kk=key_now, vv=value_now, hh=hop_index: forward_values(
                acc, query4, kk, vv, long_mask(hh), log_total
            ),
            lambda acc: acc,
            attended,
        )
    delta = row_delta(grad4, attended)
    query_gradient = jnp.zeros((LONG_DEVICE_ROWS, KVH, GROUP, HEAD_SIZE), jnp.float32)
    key_gradient = jnp.zeros((LONG_DEVICE_ROWS, KVH, HEAD_SIZE), jnp.float32)
    value_gradient = jnp.zeros((LONG_DEVICE_ROWS, KVH, HEAD_SIZE), jnp.float32)
    key_now, value_now = (key3, value3)
    for hop_index in range(SUB):
        if hop_index > 0:
            key_now, value_now = from_behind((key_now, value_now), "ctx", 1)
            key_gradient, value_gradient = shifted((key_gradient, value_gradient), "ctx", 1)

        def add_parts(totals, kk=key_now, vv=value_now, hh=hop_index):
            part_q, part_k, part_v = backward_block(
                query4, kk, vv, grad4, long_mask(hh), log_total, delta
            )
            return (totals[0] + part_q, totals[1] + part_k, totals[2] + part_v)

        query_gradient, key_gradient, value_gradient = lax.cond(
            hop_index <= member,
            add_parts,
            lambda totals: totals,
            (query_gradient, key_gradient, value_gradient),
        )
    key_gradient, value_gradient = (
        shifted(key_gradient.astype(jnp.bfloat16), "ctx", -(SUB - 1)).astype(key_gradient.dtype),
        shifted(value_gradient.astype(jnp.bfloat16), "ctx", -(SUB - 1)).astype(
            value_gradient.dtype
        ),
    )
    owner_query_gradient = jnp.concatenate(
        [
            query_gradient.reshape(LONG_DEVICE_ROWS, QUERY_HEADS * HEAD_SIZE).astype(jnp.bfloat16),
            short_dq.reshape(SHORT_DEV, QUERY_HEADS * HEAD_SIZE).astype(jnp.bfloat16),
        ],
        axis=0,
    )
    owner_key_gradient = jnp.concatenate(
        [
            key_gradient.reshape(LONG_DEVICE_ROWS, KVH * HEAD_SIZE).astype(jnp.bfloat16),
            short_dk.reshape(SHORT_DEV, KVH * HEAD_SIZE).astype(jnp.bfloat16),
        ],
        axis=0,
    )
    owner_value_gradient = jnp.concatenate(
        [
            value_gradient.reshape(LONG_DEVICE_ROWS, KVH * HEAD_SIZE).astype(jnp.bfloat16),
            short_dv.reshape(SHORT_DEV, KVH * HEAD_SIZE).astype(jnp.bfloat16),
        ],
        axis=0,
    )
    attended_all = jnp.concatenate(
        [
            attended.reshape(LONG_DEVICE_ROWS, QUERY_HEADS * HEAD_SIZE).astype(jnp.bfloat16),
            short_att.reshape(SHORT_DEV, QUERY_HEADS * HEAD_SIZE).astype(jnp.bfloat16),
        ],
        axis=0,
    )
    cot_all = jnp.concatenate([long_c, short_cotangent], axis=0)
    number_of_devices = lax.axis_size("dp") * line_size
    summed_parts = lax.psum_scatter(
        jnp.einsum("ia,ir->ar", attended_all, cot_all, preferred_element_type=jnp.float32),
        ("dp", "ctx"),
        scatter_dimension=0,
        tiled=True,
    )
    adapter_down_gradient = summed_parts * (1.0 / math.sqrt(DEVICE_ROWS * number_of_devices))
    return (owner_query_gradient, owner_key_gradient, owner_value_gradient, adapter_down_gradient)


MESH_ID = pl.DeviceIdType.MESH
F32 = jnp.float32
BF16 = jnp.bfloat16
SLOT_ROWS = 24
PAIR_ROWS = 48
ZS = 4
SCALE = 1.0 / math.sqrt(HEAD_SIZE)
EXP2_SCALE = SCALE / math.log(2.0)


def nn(a, b):
    return lax.dot_general(a, b, (((1,), (0,)), ((), ())), preferred_element_type=F32)


def nt(a, b):
    return lax.dot_general(a, b, (((1,), (1,)), ((), ())), preferred_element_type=F32)


def tn(a, b):
    return lax.dot_general(a, b, (((0,), (0,)), ((), ())), preferred_element_type=F32)


def iota(shape, dim):
    return lax.broadcasted_iota(jnp.int32, shape, dim)


def col_backward(keys_now, values_now, values_t, q_rows, g_rows, bias):
    s = nt(keys_now, q_rows) + bias
    top = jnp.max(s, axis=0, keepdims=True)
    p = jnp.exp2((s - top) * EXP2_SCALE)
    mass = jnp.sum(p, axis=0, keepdims=True)
    w = (p * (1.0 / mass)).astype(BF16)
    att_t = nn(values_t, w)
    dprob = nt(values_now, g_rows)
    w32 = w.astype(F32)
    delta = jnp.sum(w32 * dprob, axis=0, keepdims=True)
    ds = (w32 * (dprob - delta) * SCALE).astype(BF16)
    return w, att_t.astype(BF16), ds


def line_kernel(
    q_ref, k_ref, v_ref, d_ref, og_ref, down_ref, own_ref, slot_ref, len_ref,
    dq_ref, dk_ref, dv_ref, ad_ref,
    kvb, idxb, perm, bias2, pack2, unpack2, w_all, ds_all, q_all, g_all, ogs_bd, bias_s,
    og_t, packed, recv_q, part, recv_a, send_b, recv_b, ad_part, recv_ad, ad_sum, recv_ad2,
    ag_send, ag_recv, ix_send, ix_recv, q_send, q_recv, a_send, a_recv, b_send, b_recv,
    ad_send, ad_recv, ad2_send, ad2_recv,
):
    a = lax.axis_index("dp")
    c = lax.axis_index("ctx")
    z = c // 2
    core = c - 2 * z
    mate = 2 * z + 1 - core

    def sender(src, dst, ssem, rsem, dp, ctx):
        return pltpu.make_async_remote_copy(
            src_ref=src, dst_ref=dst, send_sem=ssem, recv_sem=rsem,
            device_id=(dp, ctx), device_id_type=MESH_ID,
        )

    barrier = pltpu.get_barrier_semaphore()
    for step in range(1, 8):
        pl.semaphore_signal(barrier, inc=1, device_id=(a, lax.rem(c + step, 8)), device_id_type=MESH_ID)
    for step in range(1, 4):
        pl.semaphore_signal(barrier, inc=1, device_id=(lax.rem(a + step, 4), c), device_id_type=MESH_ID)

    for k in range(KVH):
        cols = slice(k * HEAD_SIZE, (k + 1) * HEAD_SIZE)
        kvb[c, k, :, 0:HEAD_SIZE] = k_ref[0:LONG_DEVICE_ROWS, cols]
        kvb[c, k, :, HEAD_SIZE:2 * HEAD_SIZE] = v_ref[0:LONG_DEVICE_ROWS, cols]
    row16 = iota((16, NB), 0)
    own_slot = jnp.where(
        row16 == 0, own_ref[...], jnp.where(row16 == 1, slot_ref[...], 0)
    ).astype(F32).astype(BF16)
    spread = (iota((NB, 128), 0) == lax.shift_right_logical(iota((NB, 128), 1), 1)).astype(F32).astype(BF16)
    idxb[c] = nn(own_slot, spread).astype(BF16)

    pl.semaphore_wait(barrier, 10)

    def kv_copy(way, s, k):
        to = (c + 2, c - 2, mate)[way]
        return sender(kvb.at[s, k], kvb.at[s, k], ag_send.at[way, s, k], ag_recv.at[s, k], a, to)

    def ix_copy(way, s):
        to = (c + 2, c - 2, mate)[way]
        return sender(idxb.at[s], idxb.at[s], ix_send.at[way, s], ix_recv.at[s], a, to)

    def can_send(way, source_z):
        if way == 0:
            return (z < ZS - 1) & (source_z <= z)
        return (z > 0) & (source_z >= z)

    def gather_steps(copy):
        @pl.when(z < ZS - 1)
        def _():
            copy(0, c).start()

        @pl.when(z > 0)
        def _():
            copy(1, c).start()

        copy(2, c).start()

    def gather_hop(copy, hop):
        @pl.when(z >= hop)
        def _():
            s = c - 2 * hop
            copy(2, s).wait_recv()

            @pl.when(z < ZS - 1)
            def _():
                copy(0, s).start()

            copy(2, s).start()

        @pl.when(z + hop < ZS)
        def _():
            s = c + 2 * hop
            copy(2, s).wait_recv()

            @pl.when(z > 0)
            def _():
                copy(1, s).start()

            copy(2, s).start()

    def gather_end(copy):
        for zz in range(ZS):
            copy(2, 2 * zz + 1 - core).wait_recv()

    def gather_drain(copy):
        for hop in range(ZS):
            for sign in ((1,) if hop == 0 else (1, -1)):
                sz = z - sign * hop
                there = (sz >= 0) & (sz < ZS)
                s = c - 2 * sign * hop

                @pl.when(there)
                def _():
                    copy(2, s).wait_send()

                if hop == 0 or sign == 1:
                    @pl.when(there & (z < ZS - 1))
                    def _():
                        copy(0, s).wait_send()

                if hop == 0 or sign == -1:
                    @pl.when(there & (z > 0))
                    def _():
                        copy(1, s).wait_send()

    gather_steps(ix_copy)
    for k in range(KVH):
        gather_steps(lambda way, s, k=k: kv_copy(way, s, k))

    og_long = og_ref[0:LONG_DEVICE_ROWS, :]
    og_short = og_ref[LONG_DEVICE_ROWS:DEVICE_ROWS, :]
    og_t[...] = jnp.transpose(og_long.astype(F32)).astype(BF16)
    rep = ((iota((256, 32), 0) & 31) == iota((256, 32), 1)).astype(F32).astype(BF16)
    ogs_wide = nt(nt(rep, og_short).astype(BF16), rep)
    same = lax.shift_right_logical(iota((256, 256), 0), 5) == lax.shift_right_logical(iota((256, 256), 1), 5)
    ogs_bd[...] = jnp.where(same, ogs_wide, 0.0).astype(BF16)
    e0 = len_ref[0, 0]
    e1 = e0 + len_ref[0, 1]
    e2 = e1 + len_ref[0, 2]

    def segment(ids):
        return sum((ids >= e).astype(jnp.int32) for e in (e0, e1, e2))

    key_id = iota((SHORT_DEV, 256), 0)
    row_id = iota((SHORT_DEV, 256), 1) & 31
    seen = (segment(key_id) == segment(row_id)) & (key_id <= row_id)
    bias_s[...] = jnp.where(seen, 0.0, NEG_FILL)

    for hop in range(1, ZS):
        gather_hop(ix_copy, hop)
    gather_end(ix_copy)
    for k in range(KVH):
        for hop in range(1, ZS):
            gather_hop(lambda way, s, k=k: kv_copy(way, s, k), hop)

    idx = idxb[...].astype(F32)
    lane = iota((1, 128), 1)
    odd = (lane & 1).astype(F32)
    owners = [idx[s, 0:1, :] for s in range(8)]
    places = [owners[s] * 128.0 + idx[s, 1:2, :] * 2.0 + odd for s in range(8)]
    before = (iota((128, 128), 0) < iota((128, 128), 1)).astype(F32).astype(BF16)
    eight = iota((8, 128), 0).astype(F32)
    hot = jnp.concatenate([(eight == owners[s]).astype(F32) for s in range(8)], axis=0)
    counts = hot * nn(hot.astype(BF16), before)
    ranks = [jnp.sum(counts[8 * s:8 * s + 8], axis=0, keepdims=True) for s in range(8)]
    line_id = iota((1024, 128), 0).astype(F32)
    for s in range(8):
        perm[:, s * 128:(s + 1) * 128] = (line_id == places[s]).astype(F32).astype(BF16)

    mine = idxb[c].astype(F32)
    own_mine = mine[0:1, :]
    place_mine = own_mine * 128.0 + mine[1:2, :] * 2.0 + odd
    start_mine = jnp.where(own_mine >= 4.0, 512.0, 0.0)
    bias = jnp.where((line_id >= start_mine) & (line_id <= place_mine), 0.0, NEG_FILL)
    bias2[:, 0:128] = bias
    bias2[:, 128:256] = bias
    hot_mine = (eight == own_mine).astype(F32)
    rank_mine = jnp.sum(hot_mine * nn(hot_mine.astype(BF16), before), axis=0, keepdims=True)
    to_mine = own_mine * SLOT_ROWS + rank_mine
    to_two = jnp.concatenate([to_mine, to_mine], axis=1)
    block = iota((8, PAIR_ROWS, 256), 0)
    within = iota((8, PAIR_ROWS, 256), 1)
    half = (within >= SLOT_ROWS).astype(jnp.int32)
    place = (block * SLOT_ROWS + within - SLOT_ROWS * half).astype(F32)
    lane_half = lax.shift_right_logical(iota((8, PAIR_ROWS, 256), 2), 7)
    hit = (place == to_two[None]) & (half == lane_half)
    pack2[...] = hit.astype(F32).reshape(8 * PAIR_ROWS, 256).astype(BF16)

    me_f = c.astype(F32) * 128.0
    local = iota((128, 128), 0).astype(F32) + me_f
    lands = jnp.concatenate(
        [(local == places[s]).astype(F32).astype(BF16) for s in range(8)], axis=1
    )
    rank_line = jnp.concatenate(ranks, axis=1)
    from_lane = lax.shift_right_logical(iota((8, PAIR_ROWS, 1024), 2), 7) == iota((8, PAIR_ROWS, 1024), 0)
    within_f = iota((8, PAIR_ROWS, 1024), 1).astype(F32)
    for h in range(2):
        holds = (from_lane & (within_f - float(SLOT_ROWS * h) == rank_line[None])).astype(F32)
        holds = holds.reshape(8 * PAIR_ROWS, 1024).astype(BF16)
        unpack2[h * 128:(h + 1) * 128, :] = nt(lands, holds).astype(BF16)

    def head_cols(h):
        return pl.ds(pl.multiple_of(h * HEAD_SIZE, HEAD_SIZE), HEAD_SIZE)

    def grad_head(h, rows, og_rows):
        branch = nt(og_rows, down_ref[pl.ds(pl.multiple_of(h * HEAD_SIZE, HEAD_SIZE), HEAD_SIZE), :])
        return (d_ref[rows, head_cols(h)].astype(F32) + branch).astype(BF16)

    long_rows = slice(0, LONG_DEVICE_ROWS)
    short_rows = slice(LONG_DEVICE_ROWS, DEVICE_ROWS)

    def a_copy(k):
        return sender(part.at[k, 1 - core], recv_a.at[k], a_send.at[k], a_recv.at[k], a, mate)

    def b_copy(k, step):
        to = lax.rem(z + step, ZS)
        return sender(send_b.at[k, to], recv_b.at[k, z], b_send.at[k, to], b_recv.at[k, z], a, 2 * to + core)

    def b_landed(k, step):
        frm = lax.rem(z + step, ZS)
        return sender(send_b.at[k, frm], recv_b.at[k, frm], b_send.at[k, frm], b_recv.at[k, frm], a, 2 * frm + core)

    def q_copy(k, step):
        to = lax.rem(c + step, 8)
        return sender(packed.at[k, to], recv_q.at[k, c], q_send.at[k, to], q_recv.at[k, c], a, to)

    def q_landed(k, step):
        frm = lax.rem(c + step, 8)
        return sender(packed.at[k, frm], recv_q.at[k, frm], q_send.at[k, frm], q_recv.at[k, frm], a, frm)

    def ad_copy(k):
        return sender(ad_part.at[k], recv_ad.at[a], ad_send.at[k], ad_recv.at[a], k, c)

    def ad_landed(step):
        frm = lax.rem(a + step, 4)
        return sender(ad_part.at[frm], recv_ad.at[frm], ad_send.at[frm], ad_recv.at[frm], frm, c)

    def ad2_copy(step):
        to = lax.rem(c + step, 8)
        return sender(ad_sum.at[to], recv_ad2.at[c], ad2_send.at[to], ad2_recv.at[c], a, to)

    def ad2_landed(step):
        frm = lax.rem(c + step, 8)
        return sender(ad_sum.at[frm], recv_ad2.at[frm], ad2_send.at[frm], ad2_recv.at[frm], a, frm)

    def chip_sum(k):
        a_copy(k).wait_recv()
        total = part[k, core].astype(F32) + recv_a[k].astype(F32)
        send_b[k] = total.astype(BF16)
        for step in range(1, ZS):
            b_copy(k, step).start()

    def group(k, carry):
        for zz in range(ZS):
            kv_copy(2, 2 * zz + 1 - core, k).wait_recv()
        blocks = jnp.concatenate([kvb[s, k] for s in range(8)], axis=0)
        ordered = nn(perm[...], blocks)
        ordered_t = jnp.transpose(ordered)
        key_o = ordered[:, 0:128].astype(BF16)
        val_o = ordered[:, 128:256].astype(BF16)
        key_t = ordered_t[0:128].astype(BF16)
        val_t = ordered_t[128:256].astype(BF16)

        ks = k_ref[short_rows, head_cols(k)]
        vs = v_ref[short_rows, head_cols(k)]
        qs = jnp.concatenate([q_ref[short_rows, head_cols(k * GROUP + g)] for g in range(GROUP)], axis=0)
        gs = jnp.concatenate([grad_head(k * GROUP + g, short_rows, og_short) for g in range(GROUP)], axis=0)
        vs_t = jnp.transpose(vs.astype(F32)).astype(BF16)
        w, att_t, ds = col_backward(ks, vs, vs_t, qs, gs, bias_s[...])
        dqs = tn(ds, ks).astype(BF16)
        for g in range(GROUP):
            dq_ref[short_rows, head_cols(k * GROUP + g)] = dqs[g * SHORT_DEV:(g + 1) * SHORT_DEV]
        dk_ref[short_rows, head_cols(k)] = nn(ds, qs).astype(BF16)
        dv_ref[short_rows, head_cols(k)] = nn(w, gs).astype(BF16)
        ad_part[k] = nt(ogs_bd[...], att_t).reshape(GROUP, ADAPTER_RANK, HEAD_SIZE)

        for p in range(4):
            heads = (k * GROUP + 2 * p, k * GROUP + 2 * p + 1)
            qp = jnp.concatenate([q_ref[long_rows, head_cols(h)] for h in heads], axis=0)
            gp = jnp.concatenate([grad_head(h, long_rows, og_long) for h in heads], axis=0)
            w, att_t, ds = col_backward(key_o, val_o, val_t, qp, gp, bias2[...])
            cols = slice(p * 256, (p + 1) * 256)
            w_all[:, cols] = w
            ds_all[:, cols] = ds
            q_all[cols, :] = qp
            g_all[cols, :] = gp
            dq_t = nn(key_t, ds).astype(BF16)
            packed[k, :, :, p * 128:(p + 1) * 128] = (
                nt(pack2[...], dq_t).astype(BF16).reshape(8, PAIR_ROWS, HEAD_SIZE)
            )
            for h in range(2):
                ad_part[k, 2 * p + h] += nt(og_t[...], att_t[:, h * 128:(h + 1) * 128])

        for step in range(1, 8):
            q_copy(k, step).start()
        recv_q[k, c] = packed[k, c]

        dk = nn(ds_all[...], q_all[...]).astype(BF16).reshape(ZS, 2, 128, HEAD_SIZE)
        dv = nn(w_all[...], g_all[...]).astype(BF16).reshape(ZS, 2, 128, HEAD_SIZE)
        for zz in range(ZS):
            for cc in range(2):
                part[k, cc, zz, :, 0:128] = dk[zz, cc]
                part[k, cc, zz, :, 128:256] = dv[zz, cc]
        a_copy(k).start()

        @pl.when(k != a)
        def _():
            ad_copy(k).start()

        @pl.when(k > 0)
        def _():
            chip_sum(k - 1)

        return carry

    lax.fori_loop(0, KVH, group, 0)
    chip_sum(KVH - 1)

    for step in range(1, 4):
        ad_landed(step).wait_recv()
    recv_ad[a] = ad_part[a]
    total = recv_ad[0] + recv_ad[1] + recv_ad[2] + recv_ad[3]
    ad_sum[...] = total.astype(BF16)
    for step in range(1, 8):
        ad2_copy(step).start()
    recv_ad2[c] = ad_sum[c]

    def finish(k, carry):
        for step in range(1, 8):
            q_landed(k, step).wait_recv()
        rows = nn(unpack2[...], recv_q[k].reshape(8 * PAIR_ROWS, 512)).astype(BF16)
        for p in range(4):
            for h in range(2):
                dq_ref[long_rows, head_cols(k * GROUP + 2 * p + h)] = rows[
                    h * 128:(h + 1) * 128, p * 128:(p + 1) * 128
                ]
        total = send_b[k, z].astype(F32)
        for step in range(1, ZS):
            b_landed(k, step).wait_recv()
            total += recv_b[k, lax.rem(z + step, ZS)].astype(F32)
        dk_ref[long_rows, head_cols(k)] = total[:, 0:128].astype(BF16)
        dv_ref[long_rows, head_cols(k)] = total[:, 128:256].astype(BF16)
        return carry

    lax.fori_loop(0, KVH, finish, 0)

    for step in range(1, 8):
        ad2_landed(step).wait_recv()
    total = recv_ad2[0].astype(F32)
    for s in range(1, 8):
        total += recv_ad2[s].astype(F32)
    ad_ref[...] = jnp.transpose(total) * (1.0 / math.sqrt(DEVICE_ROWS * 32))

    gather_drain(ix_copy)

    def drain(k, carry):
        gather_drain(lambda way, s: kv_copy(way, s, k))
        for step in range(1, 8):
            q_copy(k, step).wait_send()
        a_copy(k).wait_send()
        for step in range(1, ZS):
            b_copy(k, step).wait_send()

        @pl.when(k != a)
        def _():
            ad_copy(k).wait_send()

        return carry

    lax.fori_loop(0, KVH, drain, 0)
    for step in range(1, 8):
        ad2_copy(step).wait_send()


def line_shards(q, k, v, d, og, down, own, slot, lengths):
    vmem = pl.BlockSpec(memory_space=pltpu.VMEM)
    smem = pl.BlockSpec(memory_space=pltpu.SMEM)
    dma = pltpu.SemaphoreType.DMA
    return pl.pallas_call(
        line_kernel,
        out_shape=(
            jax.ShapeDtypeStruct((DEVICE_ROWS, QUERY_HEADS * HEAD_SIZE), BF16),
            jax.ShapeDtypeStruct((DEVICE_ROWS, KVH * HEAD_SIZE), BF16),
            jax.ShapeDtypeStruct((DEVICE_ROWS, KVH * HEAD_SIZE), BF16),
            jax.ShapeDtypeStruct((HEAD_SIZE, ADAPTER_RANK), F32),
        ),
        in_specs=[vmem] * 8 + [smem],
        out_specs=[vmem] * 4,
        scratch_shapes=[
            pltpu.VMEM((8, KVH, 128, 256), BF16),
            pltpu.VMEM((8, 16, 128), BF16),
            pltpu.VMEM((1024, 1024), BF16),
            pltpu.VMEM((1024, 256), F32),
            pltpu.VMEM((8 * PAIR_ROWS, 256), BF16),
            pltpu.VMEM((256, 8 * PAIR_ROWS), BF16),
            pltpu.VMEM((1024, 1024), BF16),
            pltpu.VMEM((1024, 1024), BF16),
            pltpu.VMEM((1024, 128), BF16),
            pltpu.VMEM((1024, 128), BF16),
            pltpu.VMEM((256, 256), BF16),
            pltpu.VMEM((SHORT_DEV, 256), F32),
            pltpu.VMEM((ADAPTER_RANK, 128), BF16),
            pltpu.VMEM((KVH, 8, PAIR_ROWS, 512), BF16),
            pltpu.VMEM((KVH, 8, PAIR_ROWS, 512), BF16),
            pltpu.VMEM((KVH, 2, ZS, 128, 256), BF16),
            pltpu.VMEM((KVH, ZS, 128, 256), BF16),
            pltpu.VMEM((KVH, ZS, 128, 256), BF16),
            pltpu.VMEM((KVH, ZS, 128, 256), BF16),
            pltpu.VMEM((KVH, GROUP, ADAPTER_RANK, HEAD_SIZE), F32),
            pltpu.VMEM((4, GROUP, ADAPTER_RANK, HEAD_SIZE), F32),
            pltpu.VMEM((8, ADAPTER_RANK, HEAD_SIZE), BF16),
            pltpu.VMEM((8, ADAPTER_RANK, HEAD_SIZE), BF16),
            dma((3, 8, KVH)), dma((8, KVH)),
            dma((3, 8)), dma((8,)),
            dma((KVH, 8)), dma((KVH, 8)),
            dma((KVH,)), dma((KVH,)),
            dma((KVH, ZS)), dma((KVH, ZS)),
            dma((4,)), dma((4,)),
            dma((8,)), dma((8,)),
        ],
        compiler_params=pltpu.CompilerParams(
            collective_id=0, has_side_effects=True, vmem_limit_bytes=56 * 1024 * 1024
        ),
        cost_estimate=pl.CostEstimate(flops=10 ** 10, bytes_accessed=8 * 10 ** 6, transcendentals=4 * 10 ** 6),
    )(q, k, v, d, og, down, own, slot, lengths)


def solution(mesh):
    in_specs = (
        P(("dp", "ctx"), None),
        P(("dp", "ctx"), None),
        P(("dp", "ctx"), None),
        P(("dp", "ctx"), None),
        P(("dp", "ctx"), None),
        P(),
        P(("dp", "ctx"), None),
        P(("dp", "ctx"), None),
        P(("dp", "ctx"), None),
    )
    out_specs = (
        P(("dp", "ctx"), None),
        P(("dp", "ctx"), None),
        P(("dp", "ctx"), None),
        P(("dp", "ctx"), None),
    )
    body = line_shards if dict(mesh.shape) == {"dp": 4, "ctx": 8} else shards
    return jax.shard_map(body, mesh=mesh, in_specs=in_specs, out_specs=out_specs, check_vma=False)
```

```python
import math

import jax
import jax.numpy as jnp
from jax import lax
from jax.experimental import pallas as pl
from jax.experimental.pallas import tpu as pltpu
from jax.sharding import PartitionSpec as P

HEAD_SIZE = 128
QUERY_HEADS = 32
KVH = 4
GROUP = 8
ADAPTER_RANK = 32
LONG_DEVICE_ROWS = 128
SHORT_DEV = 32
SUB = 4
BLK = 2
NB = 64
DEVICE_ROWS = 160


NEG_FILL = -1e30


def from_behind(shard, axis, by):
    count = lax.axis_size(axis)
    pairs = [(i, i + by) for i in range(count) if 0 <= i + by < count]
    return lax.ppermute(shard, axis, pairs)


def shifted(block, axis, distance):
    devices = range(lax.axis_size(axis))
    route = [((i - distance) % len(devices), i) for i in devices]
    return lax.ppermute(block, axis, route)


def head_scores(query4, key3):
    raw = jnp.einsum("ikgd,jkd->kgij", query4, key3, preferred_element_type=jnp.float32)
    return raw * (1.0 / math.sqrt(query4.shape[3]))


def running_stats(state, query4, key3, visible_mask):
    best, mass = state
    raw = head_scores(query4, key3)
    fresh = jnp.maximum(best, jnp.max(jnp.where(visible_mask, raw, NEG_FILL), axis=-1))
    mass = mass * jnp.exp(best - fresh) + jnp.sum(
        jnp.where(visible_mask, jnp.exp(raw - fresh[..., None]), 0.0), axis=-1
    )
    return (fresh, mass)


def block_weights(query4, key3, visible_mask, log_total):
    raw = head_scores(query4, key3)
    return jnp.where(visible_mask, jnp.exp(raw - log_total[..., None]), 0.0).astype(jnp.bfloat16)


def forward_values(attended, query4, key3, value3, visible_mask, log_total):
    weights = block_weights(query4, key3, visible_mask, log_total)
    return attended + jnp.einsum(
        "kgij,jkd->ikgd", weights, value3, preferred_element_type=jnp.float32
    )


def backward_block(query4, key3, value3, grad4, visible_mask, log_total, delta):
    weights = block_weights(query4, key3, visible_mask, log_total)
    dprob = jnp.einsum("ikgd,jkd->kgij", grad4, value3, preferred_element_type=jnp.float32)
    dscore = (
        weights.astype(jnp.float32)
        * (dprob - delta[..., None])
        * (1.0 / math.sqrt(query4.shape[3]))
    ).astype(jnp.bfloat16)
    part_q = jnp.einsum("kgij,jkd->ikgd", dscore, key3, preferred_element_type=jnp.float32)
    part_k = jnp.einsum("kgij,ikgd->jkd", dscore, query4, preferred_element_type=jnp.float32)
    part_v = jnp.einsum("kgij,ikgd->jkd", weights, grad4, preferred_element_type=jnp.float32)
    return (part_q, part_k, part_v)


def row_delta(grad4, attended):
    return jnp.einsum("ikgd,ikgd->kgi", grad4.astype(jnp.float32), attended)


def shards(
    queries,
    keys,
    values,
    output_gradient,
    adapter_rank_cotangent,
    adapter_down_weight,
    relay_owner_index,
    relay_block_slot,
    short_rollout_lengths,
):
    line_size = lax.axis_size("ctx")
    slots_each = 3 * NB // (2 * line_size)
    owners = relay_owner_index[0]
    targets = relay_block_slot[0]
    block_ids = jnp.arange(NB, dtype=jnp.int32)
    same_owner = owners[:, None] == owners[None, :]
    earlier = block_ids[None, :] < block_ids[:, None]
    within = jnp.sum((same_owner & earlier).astype(jnp.int32), axis=1)
    position = owners * slots_each + within
    buffer_ids = jnp.arange(line_size * slots_each, dtype=jnp.int32)
    matches = position[None, :] == buffer_ids[:, None]
    filled = jnp.any(matches, axis=1)
    source_ids = jnp.sum(jnp.where(matches, block_ids[None, :], 0), axis=1)
    carried = jnp.where(filled, jnp.sum(jnp.where(matches, targets[None, :], 0), axis=1), -1)

    def packed_rows(rows_in):
        blocks = rows_in[:LONG_DEVICE_ROWS].reshape(NB, BLK, rows_in.shape[1])
        chosen = jnp.take(blocks, source_ids, axis=0)
        return jnp.where(filled[:, None, None], chosen, jnp.zeros_like(chosen))

    arrived = (
        lax.all_to_all(packed_rows(queries), "ctx", split_axis=0, concat_axis=0, tiled=True),
        lax.all_to_all(packed_rows(keys), "ctx", split_axis=0, concat_axis=0, tiled=True),
        lax.all_to_all(packed_rows(values), "ctx", split_axis=0, concat_axis=0, tiled=True),
        lax.all_to_all(
            packed_rows(output_gradient), "ctx", split_axis=0, concat_axis=0, tiled=True
        ),
        lax.all_to_all(
            packed_rows(adapter_rank_cotangent), "ctx", split_axis=0, concat_axis=0, tiled=True
        ),
        lax.all_to_all(
            carried.astype(jnp.bfloat16), "ctx", split_axis=0, concat_axis=0, tiled=True
        ),
    )
    landing = arrived[5].astype(jnp.int32)
    pick_from = jnp.sum(
        jnp.where(landing[None, :] == block_ids[:, None], buffer_ids[None, :], 0), axis=1
    )

    def unpacked(received):
        return jnp.take(received, pick_from, axis=0).reshape(LONG_DEVICE_ROWS, received.shape[2])

    long_q = unpacked(arrived[0])
    long_k = unpacked(arrived[1])
    long_v = unpacked(arrived[2])
    long_d = unpacked(arrived[3])
    long_c = unpacked(arrived[4])

    def total_grad(output_cotangent, adapter_cotangent):
        branch_choice = jnp.einsum(
            "fe,ve->fv", adapter_cotangent, adapter_down_weight, preferred_element_type=jnp.float32
        )
        return (output_cotangent.astype(jnp.float32) + branch_choice).astype(jnp.bfloat16)

    short_q = queries[LONG_DEVICE_ROWS:].reshape(SHORT_DEV, KVH, GROUP, HEAD_SIZE)
    short_k = keys[LONG_DEVICE_ROWS:].reshape(SHORT_DEV, KVH, HEAD_SIZE)
    short_v = values[LONG_DEVICE_ROWS:].reshape(SHORT_DEV, KVH, HEAD_SIZE)
    short_cotangent = adapter_rank_cotangent[LONG_DEVICE_ROWS:]
    short_g = total_grad(output_gradient[LONG_DEVICE_ROWS:], short_cotangent).reshape(
        SHORT_DEV, KVH, GROUP, HEAD_SIZE
    )
    ends = jnp.cumsum(short_rollout_lengths[0])
    short_ids = jnp.arange(SHORT_DEV, dtype=jnp.int32)
    segment = jnp.sum((ends[None, :] <= short_ids[:, None]).astype(jnp.int32), axis=1)
    short_seen = (segment[:, None] == segment[None, :]) & (short_ids[None, :] <= short_ids[:, None])
    short_best = jnp.full((KVH, GROUP, SHORT_DEV), NEG_FILL, jnp.float32)
    short_best, short_mass = running_stats(
        (short_best, jnp.zeros_like(short_best)), short_q, short_k, short_seen
    )
    short_log = short_best + jnp.log(short_mass)
    short_att = forward_values(
        jnp.zeros((SHORT_DEV, KVH, GROUP, HEAD_SIZE), jnp.float32),
        short_q,
        short_k,
        short_v,
        short_seen,
        short_log,
    )
    short_delta = row_delta(short_g, short_att)
    short_dq, short_dk, short_dv = backward_block(
        short_q, short_k, short_v, short_g, short_seen, short_log, short_delta
    )
    query4 = long_q.reshape(LONG_DEVICE_ROWS, KVH, GROUP, HEAD_SIZE)
    key3 = long_k.reshape(LONG_DEVICE_ROWS, KVH, HEAD_SIZE)
    value3 = long_v.reshape(LONG_DEVICE_ROWS, KVH, HEAD_SIZE)
    grad4 = total_grad(long_d, long_c).reshape(LONG_DEVICE_ROWS, KVH, GROUP, HEAD_SIZE)
    member = lax.axis_index("ctx") % SUB
    row_ids = jnp.arange(LONG_DEVICE_ROWS, dtype=jnp.int32)

    def long_mask(hop_index):
        source = member - hop_index
        return (source >= 0) & (
            source * LONG_DEVICE_ROWS + row_ids[None, :]
            <= member * LONG_DEVICE_ROWS + row_ids[:, None]
        )

    best = jnp.full((KVH, GROUP, LONG_DEVICE_ROWS), NEG_FILL, jnp.float32)
    mass = jnp.zeros_like(best)
    stored = []
    key_now, value_now = (key3, value3)
    for hop_index in range(SUB):
        if hop_index > 0:
            key_now, value_now = from_behind((key_now, value_now), "ctx", 1)
        stored.append((key_now, value_now))
        best, mass = lax.cond(
            hop_index <= member,
            lambda state, kk=key_now, hh=hop_index: running_stats(state, query4, kk, long_mask(hh)),
            lambda state: state,
            (best, mass),
        )
    log_total = best + jnp.log(mass)
    attended = jnp.zeros((LONG_DEVICE_ROWS, KVH, GROUP, HEAD_SIZE), jnp.float32)
    key_now, value_now = (key3, value3)
    for hop_index in range(SUB):
        if hop_index > 0:
            key_now, value_now = from_behind((key_now, value_now), "ctx", 1)
        attended = lax.cond(
            hop_index <= member,
            lambda acc, kk=key_now, vv=value_now, hh=hop_index: forward_values(
                acc, query4, kk, vv, long_mask(hh), log_total
            ),
            lambda acc: acc,
            attended,
        )
    delta = row_delta(grad4, attended)
    query_gradient = jnp.zeros((LONG_DEVICE_ROWS, KVH, GROUP, HEAD_SIZE), jnp.float32)
    key_gradient = jnp.zeros((LONG_DEVICE_ROWS, KVH, HEAD_SIZE), jnp.float32)
    value_gradient = jnp.zeros((LONG_DEVICE_ROWS, KVH, HEAD_SIZE), jnp.float32)
    key_now, value_now = (key3, value3)
    for hop_index in range(SUB):
        if hop_index > 0:
            key_now, value_now = from_behind((key_now, value_now), "ctx", 1)
            key_gradient, value_gradient = shifted((key_gradient, value_gradient), "ctx", 1)

        def add_parts(totals, kk=key_now, vv=value_now, hh=hop_index):
            part_q, part_k, part_v = backward_block(
                query4, kk, vv, grad4, long_mask(hh), log_total, delta
            )
            return (totals[0] + part_q, totals[1] + part_k, totals[2] + part_v)

        query_gradient, key_gradient, value_gradient = lax.cond(
            hop_index <= member,
            add_parts,
            lambda totals: totals,
            (query_gradient, key_gradient, value_gradient),
        )
    key_gradient, value_gradient = (
        shifted(key_gradient.astype(jnp.bfloat16), "ctx", -(SUB - 1)).astype(key_gradient.dtype),
        shifted(value_gradient.astype(jnp.bfloat16), "ctx", -(SUB - 1)).astype(
            value_gradient.dtype
        ),
    )
    owner_query_gradient = jnp.concatenate(
        [
            query_gradient.reshape(LONG_DEVICE_ROWS, QUERY_HEADS * HEAD_SIZE).astype(jnp.bfloat16),
            short_dq.reshape(SHORT_DEV, QUERY_HEADS * HEAD_SIZE).astype(jnp.bfloat16),
        ],
        axis=0,
    )
    owner_key_gradient = jnp.concatenate(
        [
            key_gradient.reshape(LONG_DEVICE_ROWS, KVH * HEAD_SIZE).astype(jnp.bfloat16),
            short_dk.reshape(SHORT_DEV, KVH * HEAD_SIZE).astype(jnp.bfloat16),
        ],
        axis=0,
    )
    owner_value_gradient = jnp.concatenate(
        [
            value_gradient.reshape(LONG_DEVICE_ROWS, KVH * HEAD_SIZE).astype(jnp.bfloat16),
            short_dv.reshape(SHORT_DEV, KVH * HEAD_SIZE).astype(jnp.bfloat16),
        ],
        axis=0,
    )
    attended_all = jnp.concatenate(
        [
            attended.reshape(LONG_DEVICE_ROWS, QUERY_HEADS * HEAD_SIZE).astype(jnp.bfloat16),
            short_att.reshape(SHORT_DEV, QUERY_HEADS * HEAD_SIZE).astype(jnp.bfloat16),
        ],
        axis=0,
    )
    cot_all = jnp.concatenate([long_c, short_cotangent], axis=0)
    number_of_devices = lax.axis_size("dp") * line_size
    summed_parts = lax.psum_scatter(
        jnp.einsum("ia,ir->ar", attended_all, cot_all, preferred_element_type=jnp.float32),
        ("dp", "ctx"),
        scatter_dimension=0,
        tiled=True,
    )
    adapter_down_gradient = summed_parts * (1.0 / math.sqrt(DEVICE_ROWS * number_of_devices))
    return (owner_query_gradient, owner_key_gradient, owner_value_gradient, adapter_down_gradient)


MESH_ID = pl.DeviceIdType.MESH
F32 = jnp.float32
BF16 = jnp.bfloat16
SLOT_ROWS = 24
PAIR_ROWS = 48
ZS = 4
SCALE = 1.0 / math.sqrt(HEAD_SIZE)
EXP2_SCALE = SCALE / math.log(2.0)


def nn(a, b):
    return lax.dot_general(a, b, (((1,), (0,)), ((), ())), preferred_element_type=F32)


def nt(a, b):
    return lax.dot_general(a, b, (((1,), (1,)), ((), ())), preferred_element_type=F32)


def tn(a, b):
    return lax.dot_general(a, b, (((0,), (0,)), ((), ())), preferred_element_type=F32)


def iota(shape, dim):
    return lax.broadcasted_iota(jnp.int32, shape, dim)


def col_backward(keys_now, values_now, values_t, q_rows, g_rows, bias, pick):
    s = nt(keys_now, q_rows) + bias
    top = jnp.max(s, axis=0, keepdims=True)
    p = jnp.exp2((s - top) * EXP2_SCALE)
    mass = jnp.sum(p, axis=0, keepdims=True)
    w = (p * (1.0 / mass)).astype(BF16)
    att_t = pick(nn(values_t, w))
    dprob = nt(values_now, g_rows)
    w32 = w.astype(F32)
    delta = jnp.sum(w32 * dprob, axis=0, keepdims=True)
    ds = (w32 * (dprob - delta) * SCALE).astype(BF16)
    return w, att_t.astype(BF16), ds


def line_kernel(
    q_ref, k_ref, v_ref, d_ref, og_ref, down_ref, own_ref, slot_ref, len_ref,
    dq_ref, dk_ref, dv_ref, ad_ref,
    kvb, idxb, perm, bias2, in_second, row_half, pack2, unpack2, w_all, ds_all, q_all, g_all, ogs_bd, bias_s,
    og_t, packed, recv_q, part, recv_a, send_b, recv_b, b_total, ad_part, recv_ad, ad_sum, recv_ad2,
    ag_send, ag_recv, ix_send, ix_recv, q_send, q_recv, a_send, a_recv, b_send, b_recv,
    ad_send, ad_recv, ad2_send, ad2_recv,
):
    a = lax.axis_index("dp")
    c = lax.axis_index("ctx")
    z = c // 2
    core = c - 2 * z
    mate = 2 * z + 1 - core

    def sender(src, dst, ssem, rsem, dp, ctx):
        return pltpu.make_async_remote_copy(
            src_ref=src, dst_ref=dst, send_sem=ssem, recv_sem=rsem,
            device_id=(dp, ctx), device_id_type=MESH_ID,
        )

    barrier = pltpu.get_barrier_semaphore()
    for step in range(1, 8):
        pl.semaphore_signal(barrier, inc=1, device_id=(a, lax.rem(c + step, 8)), device_id_type=MESH_ID)
    for step in range(1, 4):
        pl.semaphore_signal(barrier, inc=1, device_id=(lax.rem(a + step, 4), c), device_id_type=MESH_ID)

    for k in range(KVH):
        cols = slice(k * HEAD_SIZE, (k + 1) * HEAD_SIZE)
        kvb[c, k, :, 0:HEAD_SIZE] = k_ref[0:LONG_DEVICE_ROWS, cols]
        kvb[c, k, :, HEAD_SIZE:2 * HEAD_SIZE] = v_ref[0:LONG_DEVICE_ROWS, cols]
    row16 = iota((16, NB), 0)
    own_slot = jnp.where(
        row16 == 0, own_ref[...], jnp.where(row16 == 1, slot_ref[...], 0)
    ).astype(F32).astype(BF16)
    spread = (iota((NB, 128), 0) == lax.shift_right_logical(iota((NB, 128), 1), 1)).astype(F32).astype(BF16)
    idxb[c] = nn(own_slot, spread).astype(BF16)

    pl.semaphore_wait(barrier, 10)

    def kv_copy(way, s, k):
        to = (c + 2, c - 2, mate)[way]
        return sender(kvb.at[s, k], kvb.at[s, k], ag_send.at[way, s, k], ag_recv.at[s, k], a, to)

    def ix_copy(way, s):
        to = (c + 2, c - 2, mate)[way]
        return sender(idxb.at[s], idxb.at[s], ix_send.at[way, s], ix_recv.at[s], a, to)

    def can_send(way, source_z):
        if way == 0:
            return (z < ZS - 1) & (source_z <= z)
        return (z > 0) & (source_z >= z)

    def gather_steps(copy):
        @pl.when(z < ZS - 1)
        def _():
            copy(0, c).start()

        @pl.when(z > 0)
        def _():
            copy(1, c).start()

        copy(2, c).start()

    def gather_hop(copy, hop):
        @pl.when(z >= hop)
        def _():
            s = c - 2 * hop
            copy(2, s).wait_recv()

            @pl.when(z < ZS - 1)
            def _():
                copy(0, s).start()

            copy(2, s).start()

        @pl.when(z + hop < ZS)
        def _():
            s = c + 2 * hop
            copy(2, s).wait_recv()

            @pl.when(z > 0)
            def _():
                copy(1, s).start()

            copy(2, s).start()

    def gather_end(copy):
        for zz in range(ZS):
            copy(2, 2 * zz + 1 - core).wait_recv()

    def gather_drain(copy):
        for hop in range(ZS):
            for sign in ((1,) if hop == 0 else (1, -1)):
                sz = z - sign * hop
                there = (sz >= 0) & (sz < ZS)
                s = c - 2 * sign * hop

                @pl.when(there)
                def _():
                    copy(2, s).wait_send()

                if hop == 0 or sign == 1:
                    @pl.when(there & (z < ZS - 1))
                    def _():
                        copy(0, s).wait_send()

                if hop == 0 or sign == -1:
                    @pl.when(there & (z > 0))
                    def _():
                        copy(1, s).wait_send()

    def kv_chunk(k):
        return lambda way, s: kv_copy(way, s, k)

    gather_steps(ix_copy)
    gather_steps(kv_chunk(0))

    og_rows_all = jnp.transpose(og_ref[...].astype(F32)).astype(BF16)
    og_long = og_rows_all[0:LONG_DEVICE_ROWS]
    og_short = og_rows_all[LONG_DEVICE_ROWS:DEVICE_ROWS]
    og_t[...] = og_ref[:, 0:LONG_DEVICE_ROWS]
    rep = ((iota((256, 32), 0) & 31) == iota((256, 32), 1)).astype(F32).astype(BF16)
    ogs_wide = nt(nt(rep, og_short).astype(BF16), rep)
    same = lax.shift_right_logical(iota((256, 256), 0), 5) == lax.shift_right_logical(iota((256, 256), 1), 5)
    ogs_bd[...] = jnp.where(same, ogs_wide, 0.0).astype(BF16)
    e0 = len_ref[0, 0]
    e1 = e0 + len_ref[0, 1]
    e2 = e1 + len_ref[0, 2]

    def segment(ids):
        return sum((ids >= e).astype(jnp.int32) for e in (e0, e1, e2))

    key_id = iota((SHORT_DEV, 256), 0)
    row_id = iota((SHORT_DEV, 256), 1) & 31
    seen = (segment(key_id) == segment(row_id)) & (key_id <= row_id)
    bias_s[...] = jnp.where(seen, 0.0, NEG_FILL)

    def head_cols(h):
        return pl.ds(pl.multiple_of(h * HEAD_SIZE, HEAD_SIZE), HEAD_SIZE)

    def grad_head(h, rows, og_rows):
        branch = nn(og_rows, down_ref[:, head_cols(h)])
        return (d_ref[rows, head_cols(h)].astype(F32) + branch).astype(BF16)

    long_rows = slice(0, LONG_DEVICE_ROWS)
    short_rows = slice(LONG_DEVICE_ROWS, DEVICE_ROWS)

    def short_group(k):
        ks = k_ref[short_rows, head_cols(k)]
        vs = v_ref[short_rows, head_cols(k)]
        qs = jnp.concatenate([q_ref[short_rows, head_cols(k * GROUP + g)] for g in range(GROUP)], axis=0)
        gs = jnp.concatenate([grad_head(k * GROUP + g, short_rows, og_short) for g in range(GROUP)], axis=0)
        vs_t = jnp.transpose(vs.astype(F32)).astype(BF16)
        w, att_t, ds = col_backward(ks, vs, vs_t, qs, gs, bias_s[...], lambda x: x)
        dqs = tn(ds, ks).astype(BF16)
        for g in range(GROUP):
            dq_ref[short_rows, head_cols(k * GROUP + g)] = dqs[g * SHORT_DEV:(g + 1) * SHORT_DEV]
        dk_ref[short_rows, head_cols(k)] = nn(ds, qs).astype(BF16)
        dv_ref[short_rows, head_cols(k)] = nn(w, gs).astype(BF16)
        ad_part[k] = nt(ogs_bd[...], att_t).reshape(GROUP, ADAPTER_RANK, HEAD_SIZE)

    short_group(0)
    for hop in range(1, ZS):
        gather_hop(ix_copy, hop)
        gather_hop(kv_chunk(0), hop)
        short_group(hop)
    gather_steps(kv_chunk(1))
    gather_end(ix_copy)

    idx = idxb[...].astype(F32)
    lane = iota((1, 128), 1)
    odd = (lane & 1).astype(F32)
    owners = [idx[s, 0:1, :] for s in range(8)]
    places = [owners[s] * 128.0 + idx[s, 1:2, :] * 2.0 + odd for s in range(8)]
    before = (iota((128, 128), 0) < iota((128, 128), 1)).astype(F32).astype(BF16)
    eight = iota((8, 128), 0).astype(F32)
    hot = jnp.concatenate([(eight == owners[s]).astype(F32) for s in range(8)], axis=0)
    counts = hot * nn(hot.astype(BF16), before)
    ranks = [jnp.sum(counts[8 * s:8 * s + 8], axis=0, keepdims=True) for s in range(8)]
    line_id = iota((1024, 128), 0).astype(F32)
    for s in range(8):
        perm[:, s * 128:(s + 1) * 128] = (line_id == places[s]).astype(F32).astype(BF16)

    mine = idxb[c].astype(F32)
    own_mine = mine[0:1, :]
    place_mine = own_mine * 128.0 + mine[1:2, :] * 2.0 + odd
    start_mine = jnp.where(own_mine >= 4.0, 512.0, 0.0)
    at_mine = place_mine - start_mine
    bias = jnp.where(line_id[0:512] <= at_mine, 0.0, NEG_FILL)
    bias2[:, 0:128] = bias
    bias2[:, 128:256] = bias
    second = (own_mine >= 4.0).astype(F32)
    second_two = jnp.concatenate([second, second], axis=1)
    in_second[...] = jnp.broadcast_to(second_two, (128, 256))
    second_rows = jnp.transpose(jnp.broadcast_to(second, (128, 128)))
    row_half[:, 0:128] = (1.0 - second_rows).astype(BF16)
    row_half[:, 128:256] = second_rows.astype(BF16)
    hot_mine = (eight == own_mine).astype(F32)
    rank_mine = jnp.sum(hot_mine * nn(hot_mine.astype(BF16), before), axis=0, keepdims=True)
    to_mine = own_mine * SLOT_ROWS + rank_mine
    to_two = jnp.concatenate([to_mine, to_mine], axis=1)
    block = iota((8, PAIR_ROWS, 256), 0)
    within = iota((8, PAIR_ROWS, 256), 1)
    half = (within >= SLOT_ROWS).astype(jnp.int32)
    place = (block * SLOT_ROWS + within - SLOT_ROWS * half).astype(F32)
    lane_half = lax.shift_right_logical(iota((8, PAIR_ROWS, 256), 2), 7)
    hit = (place == to_two[None]) & (half == lane_half)
    pack2[...] = hit.astype(F32).reshape(8 * PAIR_ROWS, 256).astype(BF16)

    def a_copy(k):
        return sender(part.at[k, 1 - core], recv_a.at[k], a_send.at[k], a_recv.at[k], a, mate)

    def b_copy(way, k, zz):
        to = c + 2 if way == 0 else c - 2
        return sender(
            send_b.at[way, k, zz], recv_b.at[way, k, zz], b_send.at[way, k, zz], b_recv.at[way, k, zz], a, to
        )

    def b_landed(way, k, zz):
        return sender(
            send_b.at[way, k, zz], recv_b.at[way, k, zz], b_send.at[way, k, zz], b_recv.at[way, k, zz], a, mate
        )

    def q_copy(k, step):
        to = lax.rem(c + step, 8)
        return sender(packed.at[k, to], recv_q.at[k, c], q_send.at[k, to], q_recv.at[k, c], a, to)

    def q_landed(k, step):
        frm = lax.rem(c + step, 8)
        return sender(packed.at[k, frm], recv_q.at[k, frm], q_send.at[k, frm], q_recv.at[k, frm], a, frm)

    def ad_copy(k):
        return sender(ad_part.at[k], recv_ad.at[a], ad_send.at[k], ad_recv.at[a], k, c)

    def ad_landed(step):
        frm = lax.rem(a + step, 4)
        return sender(ad_part.at[frm], recv_ad.at[frm], ad_send.at[frm], ad_recv.at[frm], frm, c)

    def ad2_copy(step):
        to = lax.rem(c + step, 8)
        return sender(ad_sum.at[to], recv_ad2.at[c], ad2_send.at[to], ad2_recv.at[c], a, to)

    def ad2_landed(step):
        frm = lax.rem(c + step, 8)
        return sender(ad_sum.at[frm], recv_ad2.at[frm], ad2_send.at[frm], ad2_recv.at[frm], a, frm)

    def chip_sum(k):
        a_copy(k).wait_recv()
        part[k, core] = (part[k, core].astype(F32) + recv_a[k].astype(F32)).astype(BF16)

        @pl.when(z == 0)
        def _():
            for zz in range(1, ZS):
                send_b[0, k, zz] = part[k, core, zz]
                b_copy(0, k, zz).start()

        @pl.when(z == ZS - 1)
        def _():
            for zz in range(ZS - 1):
                send_b[1, k, zz] = part[k, core, zz]
                b_copy(1, k, zz).start()

    def line_sum(k, hop):
        def pass_on(way, zz):
            b_landed(way, k, zz).wait_recv()
            send_b[way, k, zz] = (part[k, core, zz].astype(F32) + recv_b[way, k, zz].astype(F32)).astype(BF16)
            b_copy(way, k, zz).start()

        @pl.when(z == hop)
        def _():
            for zz in range(hop + 1, ZS):
                pass_on(0, zz)

        @pl.when(z == ZS - 1 - hop)
        def _():
            for zz in range(ZS - 1 - hop):
                pass_on(1, zz)

    def group(k, carry):
        for zz in range(ZS):
            kv_copy(2, 2 * zz + 1 - core, k).wait_recv()
        blocks = jnp.concatenate([kvb[s, k] for s in range(8)], axis=0)
        ordered = nn(perm[...], blocks)
        key_w = jnp.concatenate([ordered[0:512, 0:128], ordered[512:1024, 0:128]], axis=1)
        val_w = jnp.concatenate([ordered[0:512, 128:256], ordered[512:1024, 128:256]], axis=1)
        key_t = jnp.transpose(key_w).astype(BF16)
        val_t = jnp.transpose(val_w).astype(BF16)
        key_o = key_w.astype(BF16)
        val_o = val_w.astype(BF16)
        halves = row_half[...]
        halves = jnp.concatenate([halves, halves], axis=0)

        def pick(x):
            return jnp.where(in_second[...] > 0.5, x[128:256], x[0:128])

        def widen(x):
            return jnp.concatenate([x, x], axis=1) * halves

        for p in range(4):
            heads = (k * GROUP + 2 * p, k * GROUP + 2 * p + 1)
            qp = jnp.concatenate([q_ref[long_rows, head_cols(h)] for h in heads], axis=0)
            gp = jnp.concatenate([grad_head(h, long_rows, og_long) for h in heads], axis=0)
            qp, gp = widen(qp), widen(gp)
            w, att_t, ds = col_backward(key_o, val_o, val_t, qp, gp, bias2[...], pick)
            cols = slice(p * 256, (p + 1) * 256)
            w_all[:, cols] = w
            ds_all[:, cols] = ds
            q_all[cols, :] = qp
            g_all[cols, :] = gp
            dq_t = pick(nn(key_t, ds)).astype(BF16)
            packed[k, :, :, p * 128:(p + 1) * 128] = (
                nt(pack2[...], dq_t).astype(BF16).reshape(8, PAIR_ROWS, HEAD_SIZE)
            )
            for h in range(2):
                ad_part[k, 2 * p + h] += nt(og_t[...], att_t[:, h * 128:(h + 1) * 128])

            @pl.when(k < KVH - 1)
            def _(p=p):
                if p == 0:
                    @pl.when(k < KVH - 2)
                    def _():
                        gather_steps(kv_chunk(k + 2))
                else:
                    gather_hop(kv_chunk(k + 1), p)

            @pl.when(k > 0)
            def _(p=p):
                if p == 0:
                    chip_sum(k - 1)
                else:
                    line_sum(k - 1, p)

        dk = nn(ds_all[...], q_all[...]).astype(BF16)
        dv = nn(w_all[...], g_all[...]).astype(BF16)
        for zz in range(ZS):
            for cc in range(2):
                owner = 2 * zz + cc
                rows = slice((owner % 4) * 128, (owner % 4) * 128 + 128)
                cols = slice((owner // 4) * 128, (owner // 4) * 128 + 128)
                part[k, cc, zz, :, 0:128] = dk[rows, cols]
                part[k, cc, zz, :, 128:256] = dv[rows, cols]
        a_copy(k).start()
        for step in range(1, 8):
            q_copy(k, step).start()
        recv_q[k, c] = packed[k, c]

        @pl.when(k != a)
        def _():
            ad_copy(k).start()

        return carry

    lax.fori_loop(0, KVH, group, 0)

    me_f = c.astype(F32) * 128.0
    local = iota((128, 128), 0).astype(F32) + me_f
    lands = jnp.concatenate(
        [(local == places[s]).astype(F32).astype(BF16) for s in range(8)], axis=1
    )
    rank_line = jnp.concatenate(ranks, axis=1)
    from_lane = lax.shift_right_logical(iota((8, PAIR_ROWS, 1024), 2), 7) == iota((8, PAIR_ROWS, 1024), 0)
    within_f = iota((8, PAIR_ROWS, 1024), 1).astype(F32)
    for h in range(2):
        holds = (from_lane & (within_f - float(SLOT_ROWS * h) == rank_line[None])).astype(F32)
        holds = holds.reshape(8 * PAIR_ROWS, 1024).astype(BF16)
        unpack2[h * 128:(h + 1) * 128, :] = nt(lands, holds).astype(BF16)

    chip_sum(KVH - 1)

    for step in range(1, 4):
        ad_landed(step).wait_recv()
    recv_ad[a] = ad_part[a]
    total = recv_ad[0] + recv_ad[1] + recv_ad[2] + recv_ad[3]
    ad_sum[...] = total.astype(BF16)
    for step in range(1, 8):
        ad2_copy(step).start()
    recv_ad2[c] = ad_sum[c]

    for hop in range(1, ZS):
        line_sum(KVH - 1, hop)

    def finish(k, carry):
        for step in range(1, 8):
            q_landed(k, step).wait_recv()
        rows = nn(unpack2[...], recv_q[k].reshape(8 * PAIR_ROWS, 512)).astype(BF16)
        for p in range(4):
            for h in range(2):
                dq_ref[long_rows, head_cols(k * GROUP + 2 * p + h)] = rows[
                    h * 128:(h + 1) * 128, p * 128:(p + 1) * 128
                ]
        b_total[...] = part[k, core, z].astype(F32)

        @pl.when(z > 0)
        def _():
            b_landed(0, k, z).wait_recv()
            b_total[...] += recv_b[0, k, z].astype(F32)

        @pl.when(z < ZS - 1)
        def _():
            b_landed(1, k, z).wait_recv()
            b_total[...] += recv_b[1, k, z].astype(F32)

        dk_ref[long_rows, head_cols(k)] = b_total[:, 0:128].astype(BF16)
        dv_ref[long_rows, head_cols(k)] = b_total[:, 128:256].astype(BF16)
        return carry

    lax.fori_loop(0, KVH, finish, 0)

    for step in range(1, 8):
        ad2_landed(step).wait_recv()
    total = recv_ad2[0].astype(F32)
    for s in range(1, 8):
        total += recv_ad2[s].astype(F32)
    ad_ref[...] = total * (1.0 / math.sqrt(DEVICE_ROWS * 32))

    gather_drain(ix_copy)

    def drain(k, carry):
        gather_drain(lambda way, s: kv_copy(way, s, k))
        for step in range(1, 8):
            q_copy(k, step).wait_send()
        a_copy(k).wait_send()
        for zz in range(ZS):
            @pl.when(z < zz)
            def _():
                b_copy(0, k, zz).wait_send()

            @pl.when(z > zz)
            def _():
                b_copy(1, k, zz).wait_send()

        @pl.when(k != a)
        def _():
            ad_copy(k).wait_send()

        return carry

    lax.fori_loop(0, KVH, drain, 0)
    for step in range(1, 8):
        ad2_copy(step).wait_send()


def line_shards(q, k, v, d, og, down, own, slot, lengths):
    vmem = pl.BlockSpec(memory_space=pltpu.VMEM)
    smem = pl.BlockSpec(memory_space=pltpu.SMEM)
    dma = pltpu.SemaphoreType.DMA
    dq, dk, dv, ad = pl.pallas_call(
        line_kernel,
        out_shape=(
            jax.ShapeDtypeStruct((DEVICE_ROWS, QUERY_HEADS * HEAD_SIZE), BF16),
            jax.ShapeDtypeStruct((DEVICE_ROWS, KVH * HEAD_SIZE), BF16),
            jax.ShapeDtypeStruct((DEVICE_ROWS, KVH * HEAD_SIZE), BF16),
            jax.ShapeDtypeStruct((ADAPTER_RANK, HEAD_SIZE), F32),
        ),
        in_specs=[vmem] * 8 + [smem],
        out_specs=[vmem] * 4,
        scratch_shapes=[
            pltpu.VMEM((8, KVH, 128, 256), BF16),
            pltpu.VMEM((8, 16, 128), BF16),
            pltpu.VMEM((1024, 1024), BF16),
            pltpu.VMEM((512, 256), F32),
            pltpu.VMEM((128, 256), F32),
            pltpu.VMEM((128, 256), BF16),
            pltpu.VMEM((8 * PAIR_ROWS, 256), BF16),
            pltpu.VMEM((256, 8 * PAIR_ROWS), BF16),
            pltpu.VMEM((512, 1024), BF16),
            pltpu.VMEM((512, 1024), BF16),
            pltpu.VMEM((1024, 256), BF16),
            pltpu.VMEM((1024, 256), BF16),
            pltpu.VMEM((256, 256), BF16),
            pltpu.VMEM((SHORT_DEV, 256), F32),
            pltpu.VMEM((ADAPTER_RANK, 128), BF16),
            pltpu.VMEM((KVH, 8, PAIR_ROWS, 512), BF16),
            pltpu.VMEM((KVH, 8, PAIR_ROWS, 512), BF16),
            pltpu.VMEM((KVH, 2, ZS, 128, 256), BF16),
            pltpu.VMEM((KVH, ZS, 128, 256), BF16),
            pltpu.VMEM((2, KVH, ZS, 128, 256), BF16),
            pltpu.VMEM((2, KVH, ZS, 128, 256), BF16),
            pltpu.VMEM((128, 256), F32),
            pltpu.VMEM((KVH, GROUP, ADAPTER_RANK, HEAD_SIZE), F32),
            pltpu.VMEM((4, GROUP, ADAPTER_RANK, HEAD_SIZE), F32),
            pltpu.VMEM((8, ADAPTER_RANK, HEAD_SIZE), BF16),
            pltpu.VMEM((8, ADAPTER_RANK, HEAD_SIZE), BF16),
            dma((3, 8, KVH)), dma((8, KVH)),
            dma((3, 8)), dma((8,)),
            dma((KVH, 8)), dma((KVH, 8)),
            dma((KVH,)), dma((KVH,)),
            dma((2, KVH, ZS)), dma((2, KVH, ZS)),
            dma((4,)), dma((4,)),
            dma((8,)), dma((8,)),
        ],
        compiler_params=pltpu.CompilerParams(
            collective_id=0, has_side_effects=True, vmem_limit_bytes=56 * 1024 * 1024
        ),
        cost_estimate=pl.CostEstimate(flops=10 ** 10, bytes_accessed=8 * 10 ** 6, transcendentals=4 * 10 ** 6),
    )(q, k, v, d, og.T, down.T, own, slot, lengths)
    return dq, dk, dv, ad.T


def solution(mesh):
    in_specs = (
        P(("dp", "ctx"), None),
        P(("dp", "ctx"), None),
        P(("dp", "ctx"), None),
        P(("dp", "ctx"), None),
        P(("dp", "ctx"), None),
        P(),
        P(("dp", "ctx"), None),
        P(("dp", "ctx"), None),
        P(("dp", "ctx"), None),
    )
    out_specs = (
        P(("dp", "ctx"), None),
        P(("dp", "ctx"), None),
        P(("dp", "ctx"), None),
        P(("dp", "ctx"), None),
    )
    body = line_shards if dict(mesh.shape) == {"dp": 4, "ctx": 8} else shards
    return jax.shard_map(body, mesh=mesh, in_specs=in_specs, out_specs=out_specs, check_vma=False)
```

```python
import math

import jax
import jax.numpy as jnp
from jax import lax
from jax.experimental import pallas as pl
from jax.experimental.pallas import tpu as pltpu
from jax.sharding import PartitionSpec as P

HEAD_SIZE = 128
QUERY_HEADS = 32
KVH = 4
GROUP = 8
ADAPTER_RANK = 32
LONG_DEVICE_ROWS = 128
SHORT_DEV = 32
SUB = 4
BLK = 2
NB = 64
DEVICE_ROWS = 160


NEG_FILL = -1e30


def from_behind(shard, axis, by):
    count = lax.axis_size(axis)
    pairs = [(i, i + by) for i in range(count) if 0 <= i + by < count]
    return lax.ppermute(shard, axis, pairs)


def shifted(block, axis, distance):
    devices = range(lax.axis_size(axis))
    route = [((i - distance) % len(devices), i) for i in devices]
    return lax.ppermute(block, axis, route)


def head_scores(query4, key3):
    raw = jnp.einsum("ikgd,jkd->kgij", query4, key3, preferred_element_type=jnp.float32)
    return raw * (1.0 / math.sqrt(query4.shape[3]))


def running_stats(state, query4, key3, visible_mask):
    best, mass = state
    raw = head_scores(query4, key3)
    fresh = jnp.maximum(best, jnp.max(jnp.where(visible_mask, raw, NEG_FILL), axis=-1))
    mass = mass * jnp.exp(best - fresh) + jnp.sum(
        jnp.where(visible_mask, jnp.exp(raw - fresh[..., None]), 0.0), axis=-1
    )
    return (fresh, mass)


def block_weights(query4, key3, visible_mask, log_total):
    raw = head_scores(query4, key3)
    return jnp.where(visible_mask, jnp.exp(raw - log_total[..., None]), 0.0).astype(jnp.bfloat16)


def forward_values(attended, query4, key3, value3, visible_mask, log_total):
    weights = block_weights(query4, key3, visible_mask, log_total)
    return attended + jnp.einsum(
        "kgij,jkd->ikgd", weights, value3, preferred_element_type=jnp.float32
    )


def backward_block(query4, key3, value3, grad4, visible_mask, log_total, delta):
    weights = block_weights(query4, key3, visible_mask, log_total)
    dprob = jnp.einsum("ikgd,jkd->kgij", grad4, value3, preferred_element_type=jnp.float32)
    dscore = (
        weights.astype(jnp.float32)
        * (dprob - delta[..., None])
        * (1.0 / math.sqrt(query4.shape[3]))
    ).astype(jnp.bfloat16)
    part_q = jnp.einsum("kgij,jkd->ikgd", dscore, key3, preferred_element_type=jnp.float32)
    part_k = jnp.einsum("kgij,ikgd->jkd", dscore, query4, preferred_element_type=jnp.float32)
    part_v = jnp.einsum("kgij,ikgd->jkd", weights, grad4, preferred_element_type=jnp.float32)
    return (part_q, part_k, part_v)


def row_delta(grad4, attended):
    return jnp.einsum("ikgd,ikgd->kgi", grad4.astype(jnp.float32), attended)


def shards(
    queries,
    keys,
    values,
    output_gradient,
    adapter_rank_cotangent,
    adapter_down_weight,
    relay_owner_index,
    relay_block_slot,
    short_rollout_lengths,
):
    line_size = lax.axis_size("ctx")
    slots_each = 3 * NB // (2 * line_size)
    owners = relay_owner_index[0]
    targets = relay_block_slot[0]
    block_ids = jnp.arange(NB, dtype=jnp.int32)
    same_owner = owners[:, None] == owners[None, :]
    earlier = block_ids[None, :] < block_ids[:, None]
    within = jnp.sum((same_owner & earlier).astype(jnp.int32), axis=1)
    position = owners * slots_each + within
    buffer_ids = jnp.arange(line_size * slots_each, dtype=jnp.int32)
    matches = position[None, :] == buffer_ids[:, None]
    filled = jnp.any(matches, axis=1)
    source_ids = jnp.sum(jnp.where(matches, block_ids[None, :], 0), axis=1)
    carried = jnp.where(filled, jnp.sum(jnp.where(matches, targets[None, :], 0), axis=1), -1)

    def packed_rows(rows_in):
        blocks = rows_in[:LONG_DEVICE_ROWS].reshape(NB, BLK, rows_in.shape[1])
        chosen = jnp.take(blocks, source_ids, axis=0)
        return jnp.where(filled[:, None, None], chosen, jnp.zeros_like(chosen))

    arrived = (
        lax.all_to_all(packed_rows(queries), "ctx", split_axis=0, concat_axis=0, tiled=True),
        lax.all_to_all(packed_rows(keys), "ctx", split_axis=0, concat_axis=0, tiled=True),
        lax.all_to_all(packed_rows(values), "ctx", split_axis=0, concat_axis=0, tiled=True),
        lax.all_to_all(
            packed_rows(output_gradient), "ctx", split_axis=0, concat_axis=0, tiled=True
        ),
        lax.all_to_all(
            packed_rows(adapter_rank_cotangent), "ctx", split_axis=0, concat_axis=0, tiled=True
        ),
        lax.all_to_all(
            carried.astype(jnp.bfloat16), "ctx", split_axis=0, concat_axis=0, tiled=True
        ),
    )
    landing = arrived[5].astype(jnp.int32)
    pick_from = jnp.sum(
        jnp.where(landing[None, :] == block_ids[:, None], buffer_ids[None, :], 0), axis=1
    )

    def unpacked(received):
        return jnp.take(received, pick_from, axis=0).reshape(LONG_DEVICE_ROWS, received.shape[2])

    long_q = unpacked(arrived[0])
    long_k = unpacked(arrived[1])
    long_v = unpacked(arrived[2])
    long_d = unpacked(arrived[3])
    long_c = unpacked(arrived[4])

    def total_grad(output_cotangent, adapter_cotangent):
        branch_choice = jnp.einsum(
            "fe,ve->fv", adapter_cotangent, adapter_down_weight, preferred_element_type=jnp.float32
        )
        return (output_cotangent.astype(jnp.float32) + branch_choice).astype(jnp.bfloat16)

    short_q = queries[LONG_DEVICE_ROWS:].reshape(SHORT_DEV, KVH, GROUP, HEAD_SIZE)
    short_k = keys[LONG_DEVICE_ROWS:].reshape(SHORT_DEV, KVH, HEAD_SIZE)
    short_v = values[LONG_DEVICE_ROWS:].reshape(SHORT_DEV, KVH, HEAD_SIZE)
    short_cotangent = adapter_rank_cotangent[LONG_DEVICE_ROWS:]
    short_g = total_grad(output_gradient[LONG_DEVICE_ROWS:], short_cotangent).reshape(
        SHORT_DEV, KVH, GROUP, HEAD_SIZE
    )
    ends = jnp.cumsum(short_rollout_lengths[0])
    short_ids = jnp.arange(SHORT_DEV, dtype=jnp.int32)
    segment = jnp.sum((ends[None, :] <= short_ids[:, None]).astype(jnp.int32), axis=1)
    short_seen = (segment[:, None] == segment[None, :]) & (short_ids[None, :] <= short_ids[:, None])
    short_best = jnp.full((KVH, GROUP, SHORT_DEV), NEG_FILL, jnp.float32)
    short_best, short_mass = running_stats(
        (short_best, jnp.zeros_like(short_best)), short_q, short_k, short_seen
    )
    short_log = short_best + jnp.log(short_mass)
    short_att = forward_values(
        jnp.zeros((SHORT_DEV, KVH, GROUP, HEAD_SIZE), jnp.float32),
        short_q,
        short_k,
        short_v,
        short_seen,
        short_log,
    )
    short_delta = row_delta(short_g, short_att)
    short_dq, short_dk, short_dv = backward_block(
        short_q, short_k, short_v, short_g, short_seen, short_log, short_delta
    )
    query4 = long_q.reshape(LONG_DEVICE_ROWS, KVH, GROUP, HEAD_SIZE)
    key3 = long_k.reshape(LONG_DEVICE_ROWS, KVH, HEAD_SIZE)
    value3 = long_v.reshape(LONG_DEVICE_ROWS, KVH, HEAD_SIZE)
    grad4 = total_grad(long_d, long_c).reshape(LONG_DEVICE_ROWS, KVH, GROUP, HEAD_SIZE)
    member = lax.axis_index("ctx") % SUB
    row_ids = jnp.arange(LONG_DEVICE_ROWS, dtype=jnp.int32)

    def long_mask(hop_index):
        source = member - hop_index
        return (source >= 0) & (
            source * LONG_DEVICE_ROWS + row_ids[None, :]
            <= member * LONG_DEVICE_ROWS + row_ids[:, None]
        )

    best = jnp.full((KVH, GROUP, LONG_DEVICE_ROWS), NEG_FILL, jnp.float32)
    mass = jnp.zeros_like(best)
    stored = []
    key_now, value_now = (key3, value3)
    for hop_index in range(SUB):
        if hop_index > 0:
            key_now, value_now = from_behind((key_now, value_now), "ctx", 1)
        stored.append((key_now, value_now))
        best, mass = lax.cond(
            hop_index <= member,
            lambda state, kk=key_now, hh=hop_index: running_stats(state, query4, kk, long_mask(hh)),
            lambda state: state,
            (best, mass),
        )
    log_total = best + jnp.log(mass)
    attended = jnp.zeros((LONG_DEVICE_ROWS, KVH, GROUP, HEAD_SIZE), jnp.float32)
    key_now, value_now = (key3, value3)
    for hop_index in range(SUB):
        if hop_index > 0:
            key_now, value_now = from_behind((key_now, value_now), "ctx", 1)
        attended = lax.cond(
            hop_index <= member,
            lambda acc, kk=key_now, vv=value_now, hh=hop_index: forward_values(
                acc, query4, kk, vv, long_mask(hh), log_total
            ),
            lambda acc: acc,
            attended,
        )
    delta = row_delta(grad4, attended)
    query_gradient = jnp.zeros((LONG_DEVICE_ROWS, KVH, GROUP, HEAD_SIZE), jnp.float32)
    key_gradient = jnp.zeros((LONG_DEVICE_ROWS, KVH, HEAD_SIZE), jnp.float32)
    value_gradient = jnp.zeros((LONG_DEVICE_ROWS, KVH, HEAD_SIZE), jnp.float32)
    key_now, value_now = (key3, value3)
    for hop_index in range(SUB):
        if hop_index > 0:
            key_now, value_now = from_behind((key_now, value_now), "ctx", 1)
            key_gradient, value_gradient = shifted((key_gradient, value_gradient), "ctx", 1)

        def add_parts(totals, kk=key_now, vv=value_now, hh=hop_index):
            part_q, part_k, part_v = backward_block(
                query4, kk, vv, grad4, long_mask(hh), log_total, delta
            )
            return (totals[0] + part_q, totals[1] + part_k, totals[2] + part_v)

        query_gradient, key_gradient, value_gradient = lax.cond(
            hop_index <= member,
            add_parts,
            lambda totals: totals,
            (query_gradient, key_gradient, value_gradient),
        )
    key_gradient, value_gradient = (
        shifted(key_gradient.astype(jnp.bfloat16), "ctx", -(SUB - 1)).astype(key_gradient.dtype),
        shifted(value_gradient.astype(jnp.bfloat16), "ctx", -(SUB - 1)).astype(
            value_gradient.dtype
        ),
    )
    owner_query_gradient = jnp.concatenate(
        [
            query_gradient.reshape(LONG_DEVICE_ROWS, QUERY_HEADS * HEAD_SIZE).astype(jnp.bfloat16),
            short_dq.reshape(SHORT_DEV, QUERY_HEADS * HEAD_SIZE).astype(jnp.bfloat16),
        ],
        axis=0,
    )
    owner_key_gradient = jnp.concatenate(
        [
            key_gradient.reshape(LONG_DEVICE_ROWS, KVH * HEAD_SIZE).astype(jnp.bfloat16),
            short_dk.reshape(SHORT_DEV, KVH * HEAD_SIZE).astype(jnp.bfloat16),
        ],
        axis=0,
    )
    owner_value_gradient = jnp.concatenate(
        [
            value_gradient.reshape(LONG_DEVICE_ROWS, KVH * HEAD_SIZE).astype(jnp.bfloat16),
            short_dv.reshape(SHORT_DEV, KVH * HEAD_SIZE).astype(jnp.bfloat16),
        ],
        axis=0,
    )
    attended_all = jnp.concatenate(
        [
            attended.reshape(LONG_DEVICE_ROWS, QUERY_HEADS * HEAD_SIZE).astype(jnp.bfloat16),
            short_att.reshape(SHORT_DEV, QUERY_HEADS * HEAD_SIZE).astype(jnp.bfloat16),
        ],
        axis=0,
    )
    cot_all = jnp.concatenate([long_c, short_cotangent], axis=0)
    number_of_devices = lax.axis_size("dp") * line_size
    summed_parts = lax.psum_scatter(
        jnp.einsum("ia,ir->ar", attended_all, cot_all, preferred_element_type=jnp.float32),
        ("dp", "ctx"),
        scatter_dimension=0,
        tiled=True,
    )
    adapter_down_gradient = summed_parts * (1.0 / math.sqrt(DEVICE_ROWS * number_of_devices))
    return (owner_query_gradient, owner_key_gradient, owner_value_gradient, adapter_down_gradient)


MESH_ID = pl.DeviceIdType.MESH
F32 = jnp.float32
BF16 = jnp.bfloat16
SLOT_ROWS = 24
PAIR_ROWS = 48
ZS = 4
SCALE = 1.0 / math.sqrt(HEAD_SIZE)
EXP2_SCALE = SCALE / math.log(2.0)


def nn(a, b):
    return lax.dot_general(a, b, (((1,), (0,)), ((), ())), preferred_element_type=F32)


def nt(a, b):
    return lax.dot_general(a, b, (((1,), (1,)), ((), ())), preferred_element_type=F32)


def tn(a, b):
    return lax.dot_general(a, b, (((0,), (0,)), ((), ())), preferred_element_type=F32)


def iota(shape, dim):
    return lax.broadcasted_iota(jnp.int32, shape, dim)


def col_backward(keys_now, values_now, values_t, q_rows, g_rows, bias, pick):
    s = nt(keys_now, q_rows) + bias
    top = jnp.max(s, axis=0, keepdims=True)
    p = jnp.exp2((s - top) * EXP2_SCALE)
    mass = jnp.sum(p, axis=0, keepdims=True)
    w = (p * (1.0 / mass)).astype(BF16)
    att_t = pick(nn(values_t, w))
    dprob = nt(values_now, g_rows)
    w32 = w.astype(F32)
    delta = jnp.sum(w32 * dprob, axis=0, keepdims=True)
    ds = (w32 * (dprob - delta) * SCALE).astype(BF16)
    return w, att_t.astype(BF16), ds


def line_kernel(
    q_hbm, k_ref, v_ref, d_hbm, og_ref, down_ref, own_ref, slot_ref, len_ref,
    dq_ref, dk_ref, dv_ref, ad_ref,
    q_ref, d_ref, in_sem, kvb, idxb, perm, bias2, in_second, row_half, pack2, unpack2, w_all, ds_all, q_all, g_all, ogs_bd, bias_s,
    og_t, packed, recv_q, part, recv_a, send_b, recv_b, b_total, ad_part, recv_ad, ad_sum, recv_ad2,
    ag_send, ag_recv, ix_send, ix_recv, q_send, q_recv, a_send, a_recv, b_send, b_recv,
    ad_send, ad_recv, ad2_send, ad2_recv,
):
    a = lax.axis_index("dp")
    c = lax.axis_index("ctx")
    z = c // 2
    core = c - 2 * z
    mate = 2 * z + 1 - core

    def sender(src, dst, ssem, rsem, dp, ctx):
        return pltpu.make_async_remote_copy(
            src_ref=src, dst_ref=dst, send_sem=ssem, recv_sem=rsem,
            device_id=(dp, ctx), device_id_type=MESH_ID,
        )

    load_q = pltpu.make_async_copy(q_hbm, q_ref, in_sem.at[0])
    load_d = pltpu.make_async_copy(d_hbm, d_ref, in_sem.at[1])
    load_q.start()
    load_d.start()

    barrier = pltpu.get_barrier_semaphore()
    for step in range(1, 8):
        pl.semaphore_signal(barrier, inc=1, device_id=(a, lax.rem(c + step, 8)), device_id_type=MESH_ID)
    for step in range(1, 4):
        pl.semaphore_signal(barrier, inc=1, device_id=(lax.rem(a + step, 4), c), device_id_type=MESH_ID)

    for k in range(KVH):
        cols = slice(k * HEAD_SIZE, (k + 1) * HEAD_SIZE)
        kvb[c, k, :, 0:HEAD_SIZE] = k_ref[0:LONG_DEVICE_ROWS, cols]
        kvb[c, k, :, HEAD_SIZE:2 * HEAD_SIZE] = v_ref[0:LONG_DEVICE_ROWS, cols]
    row16 = iota((16, NB), 0)
    own_slot = jnp.where(
        row16 == 0, own_ref[...], jnp.where(row16 == 1, slot_ref[...], 0)
    ).astype(F32).astype(BF16)
    spread = (iota((NB, 128), 0) == lax.shift_right_logical(iota((NB, 128), 1), 1)).astype(F32).astype(BF16)
    idxb[c] = nn(own_slot, spread).astype(BF16)

    pl.semaphore_wait(barrier, 10)

    def kv_copy(way, s, k):
        to = (c + 2, c - 2, mate)[way]
        return sender(kvb.at[s, k], kvb.at[s, k], ag_send.at[way, s, k], ag_recv.at[s, k], a, to)

    def ix_copy(way, s):
        to = (c + 2, c - 2, mate)[way]
        return sender(idxb.at[s], idxb.at[s], ix_send.at[way, s], ix_recv.at[s], a, to)

    def can_send(way, source_z):
        if way == 0:
            return (z < ZS - 1) & (source_z <= z)
        return (z > 0) & (source_z >= z)

    def gather_steps(copy):
        @pl.when(z < ZS - 1)
        def _():
            copy(0, c).start()

        @pl.when(z > 0)
        def _():
            copy(1, c).start()

        copy(2, c).start()

    def gather_hop(copy, hop):
        @pl.when(z >= hop)
        def _():
            s = c - 2 * hop
            copy(2, s).wait_recv()

            @pl.when(z < ZS - 1)
            def _():
                copy(0, s).start()

            copy(2, s).start()

        @pl.when(z + hop < ZS)
        def _():
            s = c + 2 * hop
            copy(2, s).wait_recv()

            @pl.when(z > 0)
            def _():
                copy(1, s).start()

            copy(2, s).start()

    def gather_end(copy):
        for zz in range(ZS):
            copy(2, 2 * zz + 1 - core).wait_recv()

    def gather_drain(copy):
        for hop in range(ZS):
            for sign in ((1,) if hop == 0 else (1, -1)):
                sz = z - sign * hop
                there = (sz >= 0) & (sz < ZS)
                s = c - 2 * sign * hop

                @pl.when(there)
                def _():
                    copy(2, s).wait_send()

                if hop == 0 or sign == 1:
                    @pl.when(there & (z < ZS - 1))
                    def _():
                        copy(0, s).wait_send()

                if hop == 0 or sign == -1:
                    @pl.when(there & (z > 0))
                    def _():
                        copy(1, s).wait_send()

    def kv_chunk(k):
        return lambda way, s: kv_copy(way, s, k)

    gather_steps(ix_copy)
    gather_steps(kv_chunk(0))

    og_rows_all = jnp.transpose(og_ref[...].astype(F32)).astype(BF16)
    og_long = og_rows_all[0:LONG_DEVICE_ROWS]
    og_short = og_rows_all[LONG_DEVICE_ROWS:DEVICE_ROWS]
    og_t[...] = og_ref[:, 0:LONG_DEVICE_ROWS]
    rep = ((iota((256, 32), 0) & 31) == iota((256, 32), 1)).astype(F32).astype(BF16)
    ogs_wide = nt(nt(rep, og_short).astype(BF16), rep)
    same = lax.shift_right_logical(iota((256, 256), 0), 5) == lax.shift_right_logical(iota((256, 256), 1), 5)
    ogs_bd[...] = jnp.where(same, ogs_wide, 0.0).astype(BF16)
    e0 = len_ref[0, 0]
    e1 = e0 + len_ref[0, 1]
    e2 = e1 + len_ref[0, 2]

    def segment(ids):
        return sum((ids >= e).astype(jnp.int32) for e in (e0, e1, e2))

    key_id = iota((SHORT_DEV, 256), 0)
    row_id = iota((SHORT_DEV, 256), 1) & 31
    seen = (segment(key_id) == segment(row_id)) & (key_id <= row_id)
    bias_s[...] = jnp.where(seen, 0.0, NEG_FILL)

    def head_cols(h):
        return pl.ds(pl.multiple_of(h * HEAD_SIZE, HEAD_SIZE), HEAD_SIZE)

    def grad_head(h, rows, og_rows):
        branch = nn(og_rows, down_ref[:, head_cols(h)])
        return (d_ref[rows, head_cols(h)].astype(F32) + branch).astype(BF16)

    long_rows = slice(0, LONG_DEVICE_ROWS)
    short_rows = slice(LONG_DEVICE_ROWS, DEVICE_ROWS)

    def short_group(k):
        ks = k_ref[short_rows, head_cols(k)]
        vs = v_ref[short_rows, head_cols(k)]
        qs = jnp.concatenate([q_ref[short_rows, head_cols(k * GROUP + g)] for g in range(GROUP)], axis=0)
        gs = jnp.concatenate([grad_head(k * GROUP + g, short_rows, og_short) for g in range(GROUP)], axis=0)
        vs_t = jnp.transpose(vs.astype(F32)).astype(BF16)
        w, att_t, ds = col_backward(ks, vs, vs_t, qs, gs, bias_s[...], lambda x: x)
        dqs = tn(ds, ks).astype(BF16)
        for g in range(GROUP):
            dq_ref[short_rows, head_cols(k * GROUP + g)] = dqs[g * SHORT_DEV:(g + 1) * SHORT_DEV]
        dk_ref[short_rows, head_cols(k)] = nn(ds, qs).astype(BF16)
        dv_ref[short_rows, head_cols(k)] = nn(w, gs).astype(BF16)
        ad_part[k] = nt(ogs_bd[...], att_t).reshape(GROUP, ADAPTER_RANK, HEAD_SIZE)

    load_q.wait()
    load_d.wait()
    short_group(0)
    for hop in range(1, ZS):
        gather_hop(ix_copy, hop)
        gather_hop(kv_chunk(0), hop)
        gather_steps(kv_chunk(hop))
        short_group(hop)
    gather_end(ix_copy)

    idx = idxb[...].astype(F32)
    lane = iota((1, 128), 1)
    odd = (lane & 1).astype(F32)
    owners = [idx[s, 0:1, :] for s in range(8)]
    places = [owners[s] * 128.0 + idx[s, 1:2, :] * 2.0 + odd for s in range(8)]
    before = (iota((128, 128), 0) < iota((128, 128), 1)).astype(F32).astype(BF16)
    eight = iota((8, 128), 0).astype(F32)
    hot = jnp.concatenate([(eight == owners[s]).astype(F32) for s in range(8)], axis=0)
    counts = hot * nn(hot.astype(BF16), before)
    ranks = [jnp.sum(counts[8 * s:8 * s + 8], axis=0, keepdims=True) for s in range(8)]
    line_id = iota((1024, 128), 0).astype(F32)
    for s in range(8):
        perm[:, s * 128:(s + 1) * 128] = (line_id == places[s]).astype(F32).astype(BF16)

    mine = idxb[c].astype(F32)
    own_mine = mine[0:1, :]
    place_mine = own_mine * 128.0 + mine[1:2, :] * 2.0 + odd
    start_mine = jnp.where(own_mine >= 4.0, 512.0, 0.0)
    at_mine = place_mine - start_mine
    bias = jnp.where(line_id[0:512] <= at_mine, 0.0, NEG_FILL)
    bias2[:, 0:128] = bias
    bias2[:, 128:256] = bias
    second = (own_mine >= 4.0).astype(F32)
    second_two = jnp.concatenate([second, second], axis=1)
    in_second[...] = jnp.broadcast_to(second_two, (128, 256))
    second_rows = jnp.transpose(jnp.broadcast_to(second, (128, 128)))
    row_half[:, 0:128] = (1.0 - second_rows).astype(BF16)
    row_half[:, 128:256] = second_rows.astype(BF16)
    hot_mine = (eight == own_mine).astype(F32)
    rank_mine = jnp.sum(hot_mine * nn(hot_mine.astype(BF16), before), axis=0, keepdims=True)
    to_mine = own_mine * SLOT_ROWS + rank_mine
    to_two = jnp.concatenate([to_mine, to_mine], axis=1)
    block = iota((8, PAIR_ROWS, 256), 0)
    within = iota((8, PAIR_ROWS, 256), 1)
    half = (within >= SLOT_ROWS).astype(jnp.int32)
    place = (block * SLOT_ROWS + within - SLOT_ROWS * half).astype(F32)
    lane_half = lax.shift_right_logical(iota((8, PAIR_ROWS, 256), 2), 7)
    hit = (place == to_two[None]) & (half == lane_half)
    pack2[...] = hit.astype(F32).reshape(8 * PAIR_ROWS, 256).astype(BF16)

    def a_copy(k):
        return sender(part.at[k, 1 - core], recv_a.at[k], a_send.at[k], a_recv.at[k], a, mate)

    def b_copy(way, k, zz):
        to = c + 2 if way == 0 else c - 2
        return sender(
            send_b.at[way, k, zz], recv_b.at[way, k, zz], b_send.at[way, k, zz], b_recv.at[way, k, zz], a, to
        )

    def b_landed(way, k, zz):
        return sender(
            send_b.at[way, k, zz], recv_b.at[way, k, zz], b_send.at[way, k, zz], b_recv.at[way, k, zz], a, mate
        )

    far_first = (4, 3, 5, 2, 6, 1, 7)

    def q_copy(k, part_no, step):
        to = lax.rem(c + step, 8)
        return sender(
            packed.at[k, part_no, to], recv_q.at[k, part_no, c],
            q_send.at[k, part_no, to], q_recv.at[k, part_no, c], a, to,
        )

    def q_landed(k, part_no, step):
        frm = lax.rem(c + step, 8)
        return sender(
            packed.at[k, part_no, frm], recv_q.at[k, part_no, frm],
            q_send.at[k, part_no, frm], q_recv.at[k, part_no, frm], a, frm,
        )

    def relay(k, part_no):
        for step in far_first:
            q_copy(k, part_no, step).start()
        recv_q[k, part_no, c] = packed[k, part_no, c]

    def ad_copy(k):
        return sender(ad_part.at[k], recv_ad.at[a], ad_send.at[k], ad_recv.at[a], k, c)

    def ad_landed(step):
        frm = lax.rem(a + step, 4)
        return sender(ad_part.at[frm], recv_ad.at[frm], ad_send.at[frm], ad_recv.at[frm], frm, c)

    def ad2_copy(step):
        to = lax.rem(c + step, 8)
        return sender(ad_sum.at[to], recv_ad2.at[c], ad2_send.at[to], ad2_recv.at[c], a, to)

    def ad2_landed(step):
        frm = lax.rem(c + step, 8)
        return sender(ad_sum.at[frm], recv_ad2.at[frm], ad2_send.at[frm], ad2_recv.at[frm], a, frm)

    last = KVH - 1

    def direct(step):
        to = lax.rem(z + step, ZS)
        return sender(
            part.at[last, core, to], recv_b.at[0, last, z],
            b_send.at[0, last, to], b_recv.at[0, last, z], a, 2 * to + core,
        )

    def direct_landed(step):
        frm = lax.rem(z + step, ZS)
        return sender(
            part.at[last, core, frm], recv_b.at[0, last, frm],
            b_send.at[0, last, frm], b_recv.at[0, last, frm], a, 2 * frm + core,
        )

    def two_cores(k):
        a_copy(k).wait_recv()
        part[k, core] = (part[k, core].astype(F32) + recv_a[k].astype(F32)).astype(BF16)

    def chip_sum(k):
        two_cores(k)

        @pl.when(z == 0)
        def _():
            for zz in range(ZS - 1, 0, -1):
                send_b[0, k, zz] = part[k, core, zz]
                b_copy(0, k, zz).start()

        @pl.when(z == ZS - 1)
        def _():
            for zz in range(ZS - 1):
                send_b[1, k, zz] = part[k, core, zz]
                b_copy(1, k, zz).start()

    def line_sum(k, hop):
        def pass_on(way, zz):
            b_landed(way, k, zz).wait_recv()
            send_b[way, k, zz] = (part[k, core, zz].astype(F32) + recv_b[way, k, zz].astype(F32)).astype(BF16)
            b_copy(way, k, zz).start()

        @pl.when(z == hop)
        def _():
            for zz in range(ZS - 1, hop, -1):
                pass_on(0, zz)

        @pl.when(z == ZS - 1 - hop)
        def _():
            for zz in range(ZS - 1 - hop):
                pass_on(1, zz)

    def group(k, carry):
        for zz in range(ZS):
            kv_copy(2, 2 * zz + 1 - core, k).wait_recv()
        blocks = jnp.concatenate([kvb[s, k] for s in range(8)], axis=0)
        ordered = nn(perm[...], blocks)
        key_w = jnp.concatenate([ordered[0:512, 0:128], ordered[512:1024, 0:128]], axis=1)
        val_w = jnp.concatenate([ordered[0:512, 128:256], ordered[512:1024, 128:256]], axis=1)
        key_t = jnp.transpose(key_w).astype(BF16)
        val_t = jnp.transpose(val_w).astype(BF16)
        key_o = key_w.astype(BF16)
        val_o = val_w.astype(BF16)
        halves = row_half[...]
        halves = jnp.concatenate([halves, halves], axis=0)

        def pick(x):
            return jnp.where(in_second[...] > 0.5, x[128:256], x[0:128])

        def widen(x):
            return jnp.concatenate([x, x], axis=1) * halves

        for p in range(4):
            heads = (k * GROUP + 2 * p, k * GROUP + 2 * p + 1)
            qp = jnp.concatenate([q_ref[long_rows, head_cols(h)] for h in heads], axis=0)
            gp = jnp.concatenate([grad_head(h, long_rows, og_long) for h in heads], axis=0)
            qp, gp = widen(qp), widen(gp)
            w, att_t, ds = col_backward(key_o, val_o, val_t, qp, gp, bias2[...], pick)
            cols = slice(p * 256, (p + 1) * 256)
            w_all[:, cols] = w
            ds_all[:, cols] = ds
            q_all[cols, :] = qp
            g_all[cols, :] = gp
            dq_t = pick(nn(key_t, ds)).astype(BF16)
            packed[k, p // 2, :, :, (p % 2) * 128:(p % 2 + 1) * 128] = (
                nt(pack2[...], dq_t).astype(BF16).reshape(8, PAIR_ROWS, HEAD_SIZE)
            )
            for h in range(2):
                ad_part[k, 2 * p + h] += nt(og_t[...], att_t[:, h * 128:(h + 1) * 128])

            if p == 1:
                relay(k, 0)
            @pl.when(k == 0)
            def _(p=p):
                for chunk in range(1, KVH):
                    if 1 <= p + 3 - chunk <= 3:
                        gather_hop(kv_chunk(chunk), p + 3 - chunk)

            if p == 0:
                @pl.when(k > 1)
                def _():
                    line_sum(k - 2, 2)

                @pl.when(k > 0)
                def _():
                    chip_sum(k - 1)

            if p == 2:
                @pl.when(k > 0)
                def _():
                    line_sum(k - 1, 1)

        dk = nn(ds_all[...], q_all[...]).astype(BF16)
        dv = nn(w_all[...], g_all[...]).astype(BF16)
        for zz in range(ZS):
            for cc in range(2):
                owner = 2 * zz + cc
                rows = slice((owner % 4) * 128, (owner % 4) * 128 + 128)
                cols = slice((owner // 4) * 128, (owner // 4) * 128 + 128)
                part[k, cc, zz, :, 0:128] = dk[rows, cols]
                part[k, cc, zz, :, 128:256] = dv[rows, cols]
        a_copy(k).start()

        @pl.when(k != a)
        def _():
            ad_copy(k).start()

        @pl.when(k < KVH - 1)
        def _():
            relay(k, 1)

        return carry

    gather_hop(kv_chunk(1), 1)
    lax.fori_loop(0, KVH, group, 0)
    line_sum(KVH - 2, 2)
    two_cores(last)
    for step in (2, 1, 3):
        direct(step).start()
    relay(last, 1)

    me_f = c.astype(F32) * 128.0
    local = iota((128, 128), 0).astype(F32) + me_f
    lands = jnp.concatenate(
        [(local == places[s]).astype(F32).astype(BF16) for s in range(8)], axis=1
    )
    rank_line = jnp.concatenate(ranks, axis=1)
    from_lane = lax.shift_right_logical(iota((8, PAIR_ROWS, 1024), 2), 7) == iota((8, PAIR_ROWS, 1024), 0)
    within_f = iota((8, PAIR_ROWS, 1024), 1).astype(F32)
    for h in range(2):
        holds = (from_lane & (within_f - float(SLOT_ROWS * h) == rank_line[None])).astype(F32)
        holds = holds.reshape(8 * PAIR_ROWS, 1024).astype(BF16)
        unpack2[h * 128:(h + 1) * 128, :] = nt(lands, holds).astype(BF16)

    for step in range(1, 4):
        ad_landed(step).wait_recv()
    recv_ad[a] = ad_part[a]
    total = recv_ad[0] + recv_ad[1] + recv_ad[2] + recv_ad[3]
    ad_sum[...] = total.astype(BF16)
    for step in range(1, 8):
        ad2_copy(step).start()
    recv_ad2[c] = ad_sum[c]


    def finish(k, carry):
        for part_no in range(2):
            for step in range(1, 8):
                q_landed(k, part_no, step).wait_recv()
            rows = nn(unpack2[...], recv_q[k, part_no].reshape(8 * PAIR_ROWS, 256)).astype(BF16)
            for p in range(2):
                for h in range(2):
                    dq_ref[long_rows, head_cols(k * GROUP + 4 * part_no + 2 * p + h)] = rows[
                        h * 128:(h + 1) * 128, p * 128:(p + 1) * 128
                    ]
        b_total[...] = part[k, core, z].astype(F32)

        @pl.when((z > 0) & (k < last))
        def _():
            b_landed(0, k, z).wait_recv()
            b_total[...] += recv_b[0, k, z].astype(F32)

        @pl.when((z < ZS - 1) & (k < last))
        def _():
            b_landed(1, k, z).wait_recv()
            b_total[...] += recv_b[1, k, z].astype(F32)

        @pl.when(k == last)
        def _():
            for step in range(1, ZS):
                direct_landed(step).wait_recv()
                b_total[...] += recv_b[0, last, lax.rem(z + step, ZS)].astype(F32)

        dk_ref[long_rows, head_cols(k)] = b_total[:, 0:128].astype(BF16)
        dv_ref[long_rows, head_cols(k)] = b_total[:, 128:256].astype(BF16)
        return carry

    lax.fori_loop(0, KVH, finish, 0)

    for step in range(1, 8):
        ad2_landed(step).wait_recv()
    total = recv_ad2[0].astype(F32)
    for s in range(1, 8):
        total += recv_ad2[s].astype(F32)
    ad_ref[...] = total * (1.0 / math.sqrt(DEVICE_ROWS * 32))

    gather_drain(ix_copy)

    def drain(k, carry):
        gather_drain(lambda way, s: kv_copy(way, s, k))
        for part_no in range(2):
            for step in range(1, 8):
                q_copy(k, part_no, step).wait_send()
        a_copy(k).wait_send()
        for zz in range(ZS):
            @pl.when((z < zz) & (k < last))
            def _():
                b_copy(0, k, zz).wait_send()

            @pl.when((z > zz) & (k < last))
            def _():
                b_copy(1, k, zz).wait_send()

        @pl.when(k != a)
        def _():
            ad_copy(k).wait_send()

        return carry

    lax.fori_loop(0, KVH, drain, 0)
    for step in range(1, ZS):
        direct(step).wait_send()
    for step in range(1, 8):
        ad2_copy(step).wait_send()


def line_shards(q, k, v, d, og, down, own, slot, lengths):
    vmem = pl.BlockSpec(memory_space=pltpu.VMEM)
    hbm = pl.BlockSpec(memory_space=pl.ANY)
    smem = pl.BlockSpec(memory_space=pltpu.SMEM)
    dma = pltpu.SemaphoreType.DMA
    dq, dk, dv, ad = pl.pallas_call(
        line_kernel,
        out_shape=(
            jax.ShapeDtypeStruct((DEVICE_ROWS, QUERY_HEADS * HEAD_SIZE), BF16),
            jax.ShapeDtypeStruct((DEVICE_ROWS, KVH * HEAD_SIZE), BF16),
            jax.ShapeDtypeStruct((DEVICE_ROWS, KVH * HEAD_SIZE), BF16),
            jax.ShapeDtypeStruct((ADAPTER_RANK, HEAD_SIZE), F32),
        ),
        in_specs=[hbm, vmem, vmem, hbm] + [vmem] * 4 + [smem],
        out_specs=[vmem] * 4,
        scratch_shapes=[
            pltpu.VMEM((DEVICE_ROWS, QUERY_HEADS * HEAD_SIZE), BF16),
            pltpu.VMEM((DEVICE_ROWS, QUERY_HEADS * HEAD_SIZE), BF16),
            dma((2,)),
            pltpu.VMEM((8, KVH, 128, 256), BF16),
            pltpu.VMEM((8, 16, 128), BF16),
            pltpu.VMEM((1024, 1024), BF16),
            pltpu.VMEM((512, 256), F32),
            pltpu.VMEM((128, 256), F32),
            pltpu.VMEM((128, 256), BF16),
            pltpu.VMEM((8 * PAIR_ROWS, 256), BF16),
            pltpu.VMEM((256, 8 * PAIR_ROWS), BF16),
            pltpu.VMEM((512, 1024), BF16),
            pltpu.VMEM((512, 1024), BF16),
            pltpu.VMEM((1024, 256), BF16),
            pltpu.VMEM((1024, 256), BF16),
            pltpu.VMEM((256, 256), BF16),
            pltpu.VMEM((SHORT_DEV, 256), F32),
            pltpu.VMEM((ADAPTER_RANK, 128), BF16),
            pltpu.VMEM((KVH, 2, 8, PAIR_ROWS, 256), BF16),
            pltpu.VMEM((KVH, 2, 8, PAIR_ROWS, 256), BF16),
            pltpu.VMEM((KVH, 2, ZS, 128, 256), BF16),
            pltpu.VMEM((KVH, ZS, 128, 256), BF16),
            pltpu.VMEM((2, KVH, ZS, 128, 256), BF16),
            pltpu.VMEM((2, KVH, ZS, 128, 256), BF16),
            pltpu.VMEM((128, 256), F32),
            pltpu.VMEM((KVH, GROUP, ADAPTER_RANK, HEAD_SIZE), F32),
            pltpu.VMEM((4, GROUP, ADAPTER_RANK, HEAD_SIZE), F32),
            pltpu.VMEM((8, ADAPTER_RANK, HEAD_SIZE), BF16),
            pltpu.VMEM((8, ADAPTER_RANK, HEAD_SIZE), BF16),
            dma((3, 8, KVH)), dma((8, KVH)),
            dma((3, 8)), dma((8,)),
            dma((KVH, 2, 8)), dma((KVH, 2, 8)),
            dma((KVH,)), dma((KVH,)),
            dma((2, KVH, ZS)), dma((2, KVH, ZS)),
            dma((4,)), dma((4,)),
            dma((8,)), dma((8,)),
        ],
        compiler_params=pltpu.CompilerParams(
            collective_id=0, has_side_effects=True, vmem_limit_bytes=56 * 1024 * 1024
        ),
        cost_estimate=pl.CostEstimate(flops=10 ** 10, bytes_accessed=8 * 10 ** 6, transcendentals=4 * 10 ** 6),
    )(q, k, v, d, og.T, down.T, own, slot, lengths)
    return dq, dk, dv, ad.T


def solution(mesh):
    in_specs = (
        P(("dp", "ctx"), None),
        P(("dp", "ctx"), None),
        P(("dp", "ctx"), None),
        P(("dp", "ctx"), None),
        P(("dp", "ctx"), None),
        P(),
        P(("dp", "ctx"), None),
        P(("dp", "ctx"), None),
        P(("dp", "ctx"), None),
    )
    out_specs = (
        P(("dp", "ctx"), None),
        P(("dp", "ctx"), None),
        P(("dp", "ctx"), None),
        P(("dp", "ctx"), None),
    )
    body = line_shards if dict(mesh.shape) == {"dp": 4, "ctx": 8} else shards
    return jax.shard_map(body, mesh=mesh, in_specs=in_specs, out_specs=out_specs, check_vma=False)
```
